32 devices in a mesh: ha: 4 (over z), wa: 8 (over y, x, core).
Axes of the slice: x: 2, y: 2, z: 4, core: 2. Of those that a mesh axis runs over, the one named last changes fastest.
Arguments:
- queries: bfloat16 [4, 8, 384, 1536], P('ha', 'wa'), may hold values from -15 to 15
- keys_values: bfloat16 [4, 8, 3, 2, 384, 1536], P('ha', 'wa'), may hold values from -9 to 9
- far_offsets: int32 [8, 4, 12, 2], P('wa', 'ha'), may hold values from 0 to 6, all different within a row; in each aligned block of 12 rows (0 to 11, 12 to 23, ..., all dimensions but the last counted through in order) at most 5 rows name the same one
Outputs:
- attended: bfloat16 [4, 8, 384, 1536], P('ha', 'wa')
The draws below stay inside these ranges and needn't reach their ends.
Inputs may be any that keep to these rules, and one draw needn't show every extreme that they name: `far_offsets`: within the rows of one device (one tile column w, its 1 tile rows, all heads) each offset is named by at most 5 of those rows; each row names 2 different offsets.
All inputs are finite; a program needn't handle non-finite values.
Results may differ from the reference program's by a relative error of at most 0.0048.
Values may be sent and summed in bfloat16 or wider, within the bound.
No kernel may reach another device: no remote copies, remote signals or barrier semaphores. Data moves between devices by JAX's collectives and lax.ppermute only.
A program may use at most 320 MiB of HBM per device.

```python
import math
import jax
import jax.numpy as jnp
import numpy as np
from jax import lax

HEADS = 12
HD = 128
TILE = 384
TT = 3
FAR = 2
TH_DEV = 1
GH = 4
GW = 8
SPAN = 7
CAP = 5


def draw_queries(key, part):
    shape = (GH, GW, TILE, HEADS * HD)
    base = jnp.clip(jax.random.normal(jax.random.fold_in(key, 1), shape, jnp.float32), -6.0, 6.0)
    return base.astype(jnp.bfloat16)


def draw_keys_values(key, part):
    shape = (GH, GW, TT, 2, TILE, HEADS * HD)
    base = jnp.clip(jax.random.normal(jax.random.fold_in(key, 2), shape, jnp.float32), -6.0, 6.0)
    return base.astype(jnp.bfloat16)


def assign_block(stream_key, own, number, rows, count, top, bound, lean):
    ranking = jax.random.permutation(stream_key, count)
    heavy_load, common = portions_of(count, rows * top, bound, lean, True), portions_of(count, rows * top, bound, lean, False)
    places = jnp.arange(count)

    def named(lengths, turn):
        used = int((lengths > 0).sum())
        fixed = max(1, used // 4)
        passed = fixed + (places - fixed + turn * (used - fixed)) % max(1, count - fixed)
        return jnp.zeros((count,), jnp.int32).at[ranking[jnp.where(places < fixed, places, passed)]].set(jnp.asarray(lengths, jnp.int32))

    lengths = jnp.where(number % 4 == 0, named(heavy_load, number // 4), named(common, number - number // 4 - 1))
    mixed = jax.random.permutation(jax.random.fold_in(own, 3), count)
    source_of, sink = mixed[0:count // 2 * 2:2], mixed[1:count // 2 * 2:2]
    room = jnp.minimum(lengths[source_of] - 1, bound - lengths[sink]) // 2
    room = jnp.where((source_of == ranking[0]) | (sink == ranking[0]) | (lengths[sink] == 0), 0, jnp.maximum(room, 0))
    passed = jax.random.randint(jax.random.fold_in(own, 4), (count // 2,), 0, 1 << 20) % (room + 1)
    lengths = lengths.at[source_of].add(-passed).at[sink].add(passed)
    members = jnp.searchsorted(jnp.cumsum(lengths), jnp.arange(rows * top), side="right").astype(jnp.int32)
    table = members.reshape(top, rows).T
    table = table[jax.random.permutation(jax.random.fold_in(own, 1), rows)]
    turn = jax.random.randint(jax.random.fold_in(own, 2), (rows, 1), 0, top)
    return jnp.take_along_axis(table, (jnp.arange(top)[None, :] + turn) % top, axis=1)


def portions_of(number_of, total, reach, skew, full):
    portions = [(1 << 20) // math.isqrt(standing ** skew) + 1 for standing in range(1, number_of + 1)]
    largest = reach if full else min(reach, max(-(-total // number_of), total * portions[0] // sum(portions)))
    least = 1 if total - largest >= number_of - 1 else 0
    holding, spare = [largest] + [least] * (number_of - 1), total - largest - least * (number_of - 1)
    while spare > 0:
        candidates = [i for i in range(1, number_of) if holding[i] < largest] or [i for i in range(1, number_of) if holding[i] < reach]
        pool, remaining = sum([portions[i] for i in candidates]), spare
        for i in candidates:
            addition = min(reach - holding[i], max(1, remaining * portions[i] // pool), spare)
            holding[i] = holding[i] + addition
            spare = spare - addition
    return np.array(holding)


def setup_inputs(seed: int = 0) -> dict:
    key_of = jax.random.split(jax.random.key(seed), 4)
    queries = draw_queries(jax.random.fold_in(key_of[3], 71), 0)
    keys_values = draw_keys_values(jax.random.fold_in(key_of[3], 71), 0)
    far_offsets_keys = jax.random.split(jax.random.fold_in(key_of[2], 1), GW * GH * HEADS // (TH_DEV * HEADS))
    far_offsets_turns = jax.random.permutation(jax.random.fold_in(key_of[2], 3), GW * GH * HEADS // (TH_DEV * HEADS))
    far_offsets = jax.vmap(lambda own, number: assign_block(jax.random.fold_in(key_of[2], 2), own, number, TH_DEV * HEADS, SPAN, FAR, CAP, 2))(far_offsets_keys, far_offsets_turns).reshape((GW, GH, HEADS, FAR))
    return {"queries": queries, "keys_values": keys_values, "far_offsets": far_offsets}


def attend(head_queries, key_tiles, value_tiles, key_mask):
    score_scale = 1.0 / (HD ** 0.5)
    scores = jnp.einsum("iqd,ikd->iqk", head_queries.astype(jnp.float32), key_tiles.astype(jnp.float32)) * score_scale
    scores = jnp.where(key_mask, scores, -1e30)
    peak_score = jnp.max(scores, axis=2, keepdims=True)
    weights = jnp.exp(scores - peak_score)
    totals = jnp.sum(weights, axis=2, keepdims=True)
    rounded = lax.optimization_barrier(weights.astype(jnp.bfloat16)).astype(jnp.float32)
    summed = jnp.einsum("iqk,ikd->iqd", rounded, value_tiles.astype(jnp.float32))
    return (summed / totals).astype(jnp.bfloat16)


def reference(queries, keys_values, far_offsets):
    padded = jnp.pad(keys_values, ((1, 1), (1, 1), (0, 0), (0, 0), (0, 0), (0, 0)))
    columns = jnp.arange(GW, dtype=jnp.int32)
    steps_three = jnp.arange(3, dtype=jnp.int32)

    def one_row(tile_row):
        row_slab = lax.dynamic_slice_in_dim(padded, tile_row, 3, 0)
        row_tiles = lax.dynamic_index_in_dim(keys_values, tile_row, 0, keepdims=False)
        row_queries = lax.dynamic_index_in_dim(queries, tile_row, 0, keepdims=False)
        offset_rows = lax.dynamic_index_in_dim(far_offsets, tile_row, 1, keepdims=False)
        row_inside = (tile_row + steps_three - 1 >= 0) & (tile_row + steps_three - 1 < GH)
        col_inside = (columns[:, None] + steps_three[None, :] - 1 >= 0) & (columns[:, None] + steps_three[None, :] - 1 < GW)
        inside = row_inside[None, :, None] & col_inside[:, None, :]
        key_mask = jnp.concatenate([jnp.repeat(inside.reshape(GW, 9), TT * TILE, axis=1), jnp.ones((GW, FAR * TILE), dtype=bool)], axis=1)[:, None, :]

        def one_head(head_index):
            head_queries = lax.dynamic_slice_in_dim(row_queries, head_index * HD, HD, 2)
            head_slab = lax.dynamic_slice_in_dim(row_slab, head_index * HD, HD, 5)
            window = jnp.stack([head_slab[:, col_step:col_step + GW] for col_step in range(3)], axis=2)
            window = jnp.transpose(window, (1, 0, 2, 3, 4, 5, 6))
            head_offsets = jnp.take(offset_rows, head_index, axis=1)
            source = ((columns[:, None] + 1 + head_offsets) % GW).astype(jnp.int32)
            head_tiles = lax.dynamic_slice_in_dim(row_tiles, head_index * HD, HD, 4)[:, 1]
            far_tiles = head_tiles[source]
            key_tiles = jnp.concatenate([window[:, :, :, :, 0].reshape(GW, 9 * TT * TILE, HD), far_tiles[:, :, 0].reshape(GW, FAR * TILE, HD)], axis=1)
            value_tiles = jnp.concatenate([window[:, :, :, :, 1].reshape(GW, 9 * TT * TILE, HD), far_tiles[:, :, 1].reshape(GW, FAR * TILE, HD)], axis=1)
            return attend(head_queries, key_tiles, value_tiles, key_mask)

        per_head = lax.map(one_head, jnp.arange(HEADS, dtype=jnp.int32))
        return jnp.transpose(per_head, (1, 2, 0, 3)).reshape(GW, TILE, HEADS * HD)

    return lax.map(one_row, jnp.arange(GH, dtype=jnp.int32))
```

```python
import functools

import jax
import jax.numpy as jnp
from jax import lax
from jax.experimental import pallas as pl
from jax.experimental.pallas import tpu as pltpu
from jax.sharding import PartitionSpec as P

HEADS = 12
HD = 128
TILE = 384
TT = 3
FAR = 2
NEG = -1e30
SCALE2 = 1.4426950408889634 / HD**0.5
VMEM = 48 * 2**20


def pad8(n):
    return -(-n // 8) * 8


def attention(q, keys, values):
    scores = [
        lax.dot_general(q, k, (((1,), (1,)), ((), ())), preferred_element_type=jnp.float32)
        for k in keys
    ]
    peak = functools.reduce(jnp.maximum, [jnp.max(s, axis=1, keepdims=True) for s in scores])
    weights = [jnp.exp2((s - peak) * SCALE2) for s in scores]
    total = functools.reduce(jnp.add, [jnp.sum(w, axis=1, keepdims=True) for w in weights])
    summed = functools.reduce(
        jnp.add,
        [
            jnp.dot(w.astype(jnp.bfloat16), v, preferred_element_type=jnp.float32)
            for w, v in zip(weights, values)
        ],
    )
    return summed, peak, total


def window_kernel(jobs, n_q, n_kv, nh, flags, *refs):
    q_refs = refs[:n_q]
    kv_refs = refs[n_q : n_q + n_kv]
    outs = refs[n_q + n_kv : n_q + n_kv + 2 * len(jobs)]
    logs = refs[n_q + n_kv + 2 * len(jobs) :]
    head = pl.program_id(0)
    lane = lax.broadcasted_iota(jnp.int32, (TILE, HD), 1)
    for number, (qi, kvs, flag) in enumerate(jobs):
        o_ref, lse_ref, log_ref = outs[2 * number], outs[2 * number + 1], logs[number]

        @pl.when(flags[flag] != 0)
        def _(qi=qi, kvs=kvs, o_ref=o_ref, lse_ref=lse_ref, log_ref=log_ref):
            keys = [kv_refs[i][t, 0] for i in kvs for t in range(TT)]
            values = [kv_refs[i][t, 1] for i in kvs for t in range(TT)]
            summed, peak, total = attention(q_refs[qi][...], keys, values)
            o_ref[...] = (summed / total).astype(o_ref.dtype)
            log_ref[...] = jnp.where(lane == head, peak * SCALE2 + jnp.log2(total), log_ref[...])

            @pl.when(head == nh - 1)
            def _():
                lse_ref[...] = log_ref[...].T[: lse_ref.shape[0]]


def window(name, flags, qs, kvs, jobs, h0, nh, q_base, out_types):
    rows = pad8(nh)
    specs = [pl.BlockSpec(memory_space=pltpu.SMEM)]
    specs += [
        pl.BlockSpec((TILE, HD), functools.partial(lambda h, d: (0, h + d), d=h0 - b)) for b in q_base
    ]
    specs += [pl.BlockSpec((TT, 2, TILE, HD), lambda h: (0, 0, 0, h + h0)) for _ in kvs]
    out_specs, out_shape = [], []
    for t in out_types:
        out_specs += [
            pl.BlockSpec((TILE, HD), lambda h: (0, h)),
            pl.BlockSpec((rows, TILE), lambda h: (0, 0)),
        ]
        out_shape += [
            jax.ShapeDtypeStruct((TILE, nh * HD), t),
            jax.ShapeDtypeStruct((rows, TILE), jnp.float32),
        ]
    pairs = sum(len(j[1]) for j in jobs) * TT * nh
    res = pl.pallas_call(
        functools.partial(window_kernel, jobs, len(qs), len(kvs), nh),
        grid=(nh,),
        in_specs=specs,
        out_specs=out_specs,
        out_shape=out_shape,
        scratch_shapes=[pltpu.VMEM((TILE, HD), jnp.float32) for _ in jobs],
        compiler_params=pltpu.CompilerParams(vmem_limit_bytes=VMEM),
        cost_estimate=pl.CostEstimate(
            flops=pairs * TILE * TILE * HD * 4 * 3,
            bytes_accessed=len(kvs) * nh * TT * 2 * TILE * HD * 2,
            transcendentals=pairs * TILE * TILE,
        ),
        name=name,
    )(flags, *qs, *kvs)
    return [(res[2 * i], res[2 * i + 1]) for i in range(len(jobs))]


def column(lse_ref, head):
    row = lse_ref[pl.ds(head, 1), :]
    return jnp.broadcast_to(row, (HD, TILE)).T


def merge_parts(parts):
    top = functools.reduce(jnp.maximum, [p[1] for p in parts])
    scales = [jnp.exp2(p[1] - top) for p in parts]
    total = functools.reduce(jnp.add, scales)
    summed = functools.reduce(
        jnp.add, [p[0].astype(jnp.float32) * s for p, s in zip(parts, scales)]
    )
    return summed, top, total


def merge_kernel(part_flags, nh, flags, *refs):
    n = len(part_flags)
    o_ref, lse_ref, log_ref = refs[2 * n :]
    head = pl.program_id(0)
    lane = lax.broadcasted_iota(jnp.int32, (TILE, HD), 1)
    parts = [
        (refs[2 * i][...], jnp.where(flags[f] != 0, column(refs[2 * i + 1], head), NEG))
        for i, f in enumerate(part_flags)
    ]
    summed, top, total = merge_parts(parts)
    o_ref[...] = (summed / total).astype(o_ref.dtype)
    log_ref[...] = jnp.where(lane == head, top + jnp.log2(total), log_ref[...])

    @pl.when(head == nh - 1)
    def _():
        lse_ref[...] = log_ref[...].T[: lse_ref.shape[0]]


def merge(name, flags, parts, part_flags, nh):
    rows = pad8(nh)
    o_spec = pl.BlockSpec((TILE, HD), lambda h: (0, h))
    l_spec = pl.BlockSpec((rows, TILE), lambda h: (0, 0))
    return pl.pallas_call(
        functools.partial(merge_kernel, part_flags, nh),
        grid=(nh,),
        in_specs=[pl.BlockSpec(memory_space=pltpu.SMEM)] + [o_spec, l_spec] * len(parts),
        out_specs=[o_spec, l_spec],
        out_shape=[
            jax.ShapeDtypeStruct((TILE, nh * HD), jnp.bfloat16),
            jax.ShapeDtypeStruct((rows, TILE), jnp.float32),
        ],
        scratch_shapes=[pltpu.VMEM((TILE, HD), jnp.float32)],
        compiler_params=pltpu.CompilerParams(vmem_limit_bytes=VMEM),
        cost_estimate=pl.CostEstimate(
            flops=TILE * HD * nh * 16, bytes_accessed=TILE * HD * nh * 12, transcendentals=0
        ),
        name=name,
    )(flags, *[a for p in parts for a in p])


def final_kernel(part_specs, n_tiles, groups, flags, places, q_ref, *refs):
    n_arrays = sum(2 * (groups if cut else 1) for _, cut in part_specs)
    arrays, tiles = refs[:n_arrays], refs[n_arrays : n_arrays + n_tiles]
    out_ref, buffer, sems = refs[n_arrays + n_tiles :]
    head = pl.program_id(0)
    per = HEADS // groups

    @pl.when(head == 0)
    def _():
        @pl.loop(0, HEADS * FAR)
        def _(i):
            cols = pl.ds(pl.multiple_of(i // FAR * HD, HD), HD)
            for d, tile in enumerate(tiles):

                @pl.when(places[i] == d)
                def _(tile=tile):
                    pltpu.make_async_copy(
                        tile.at[:, :, cols], buffer.at[i], sems.at[i]
                    ).start()

    for f in range(FAR):
        i = head * FAR + f
        pltpu.make_async_copy(buffer.at[i], buffer.at[i], sems.at[i]).wait()
    keys = [buffer[head * FAR + f, 0] for f in range(FAR)]
    values = [buffer[head * FAR + f, 1] for f in range(FAR)]
    summed, peak, total = attention(q_ref[...], keys, values)

    def finish(group):
        parts = [(summed / total, jnp.broadcast_to(peak * SCALE2 + jnp.log2(total), (TILE, HD)))]
        at = 0
        for flag, cut in part_specs:
            pick = at + (2 * group if cut else 0)
            at += 2 * (groups if cut else 1)
            log = column(arrays[pick + 1], head - group * per if cut else head)
            parts.append((arrays[pick][...], jnp.where(flags[flag] != 0, log, NEG)))
        merged, _, scale = merge_parts(parts)
        out_ref[...] = (merged / scale).astype(out_ref.dtype)

    for group in range(groups):

        @pl.when(head // per == group)
        def _(group=group):
            finish(group)


def final(flags, places, q, parts, tiles, groups):
    per = HEADS // groups
    specs, arrays, part_specs = [], [], []
    for flag, pairs in parts:
        cut = len(pairs) > 1 or groups == 1
        part_specs.append((flag, cut))
        for group, (o, lse) in enumerate(pairs):
            low = group * per if cut else 0
            high = per - 1 if cut else HEADS - 1
            specs += [
                pl.BlockSpec(
                    (TILE, HD),
                    functools.partial(
                        lambda h, low, high: (0, jnp.clip(h - low, 0, high)), low=low, high=high
                    ),
                ),
                pl.BlockSpec(lse.shape, lambda h: (0, 0)),
            ]
            arrays += [o, lse]
    block = pl.BlockSpec((TILE, HD), lambda h: (0, h))
    return pl.pallas_call(
        functools.partial(final_kernel, part_specs, len(tiles), groups),
        grid=(HEADS,),
        in_specs=[pl.BlockSpec(memory_space=pltpu.SMEM)] * 2
        + [block]
        + specs
        + [pl.BlockSpec(memory_space=pl.ANY)] * len(tiles),
        out_specs=block,
        out_shape=jax.ShapeDtypeStruct((TILE, HEADS * HD), jnp.bfloat16),
        scratch_shapes=[
            pltpu.VMEM((HEADS * FAR, 2, TILE, HD), jnp.bfloat16),
            pltpu.SemaphoreType.DMA((HEADS * FAR,)),
        ],
        compiler_params=pltpu.CompilerParams(vmem_limit_bytes=VMEM),
        cost_estimate=pl.CostEstimate(
            flops=HEADS * FAR * TILE * TILE * HD * 4 * 3,
            bytes_accessed=HEADS * FAR * 2 * TILE * HD * 2,
            transcendentals=HEADS * FAR * TILE * TILE,
        ),
        name="far_and_merge",
    )(flags, places, q, *arrays, *tiles)


def send(value, axis, perm):
    return jax.tree.map(lambda a: lax.ppermute(a, axis, perm), value)


def on_device(queries, keys_values, far_offsets):
    width, height = lax.axis_size("wa"), lax.axis_size("ha")
    col, row = lax.axis_index("wa"), lax.axis_index("ha")
    groups = 2
    per = HEADS // groups
    up = [(i, i + 1) for i in range(height - 1)]
    down = [(j, i) for i, j in up]
    mate = [(i, i ^ 1) for i in range(width)]
    across = [(i, i + 1) for i in range(1, width - 1, 2)]
    across = across + [(j, i) for i, j in across]

    q = queries.reshape(TILE, HEADS * HD)
    kv = keys_values.reshape(TT, 2, TILE, HEADS * HD)

    lo, hi = row > 0, row < height - 1
    side = (col > 0) & (col < width - 1)
    flags = jnp.stack([row >= 0, lo, hi, side, side & lo, side & hi]).astype(jnp.int32)
    owners = (col + 1 + far_offsets.reshape(-1)) % width
    places = (owners ^ col).astype(jnp.int32)

    kv_mate = send(kv, "wa", mate)
    q_lo = send(q, "ha", up)
    q_hi = send(q, "ha", down)
    q_side = send(q, "wa", across)
    qs_lo = send(q_side, "ha", up)
    qs_hi = send(q_side, "ha", down)

    tiles = {0: kv[1]}
    bit = 2
    while bit < width:
        hop = [(i, i ^ bit) for i in range(width)]
        for have in sorted(tiles):
            tiles[have | bit] = send(tiles[have], "wa", hop)
        bit *= 2
    for have in sorted(tiles):
        tiles[have | 1] = kv_mate[1] if have == 0 else send(tiles[have], "wa", mate)
    tiles = [tiles[d] for d in range(width)]

    bf, f32 = jnp.bfloat16, jnp.float32
    (own_own,) = window("own", flags, [q], [kv], [(0, (0,), 0)], 0, HEADS, [0], [f32])
    (own_mate,) = window("mate", flags, [q], [kv_mate], [(0, (0,), 0)], 0, HEADS, [0], [f32])
    from_lo, from_hi, side_parts = [], [], []
    for g in range(groups):
        o_lo, o_hi = window(
            "rows", flags, [q_lo, q_hi], [kv, kv_mate],
            [(0, (0, 1), 1), (1, (0, 1), 2)], g * per, per, [0, 0], [bf, bf],
        )
        from_lo.append(send(o_hi, "ha", up))
        from_hi.append(send(o_lo, "ha", down))
    for g in range(groups):
        s_lo, s_hi, s_own = window(
            "side", flags, [qs_lo, qs_hi, q_side], [kv],
            [(0, (0,), 4), (1, (0,), 5), (2, (0,), 3)], g * per, per, [0, 0, 0], [bf, bf, f32],
        )
        s_from_lo = send(s_hi, "ha", up)
        s_from_hi = send(s_lo, "ha", down)
        merged = merge("side_merge", flags, [s_own, s_from_lo, s_from_hi], [3, 4, 5], per)
        side_parts.append(send(tuple(merged), "wa", across))
    out = final(
        flags, places, q,
        [(0, [own_own]), (0, [own_mate]), (1, from_lo), (2, from_hi), (3, side_parts)],
        tiles, groups,
    )
    return out.reshape(queries.shape)


def solution(mesh):
    placed = (
        P("ha", "wa", None, None),
        P("ha", "wa", None, None, None, None),
        P("wa", "ha", None, None),
    )
    return jax.shard_map(
        on_device, mesh=mesh, in_specs=placed, out_specs=P("ha", "wa", None, None), check_vma=False
    )
```

```python
import functools

import jax
import jax.numpy as jnp
from jax import lax
from jax.experimental import pallas as pl
from jax.experimental.pallas import tpu as pltpu
from jax.sharding import PartitionSpec as P

HEADS = 12
HD = 128
TILE = 384
TT = 3
FAR = 2
NEG = -1e30
SCALE2 = 1.4426950408889634 / HD**0.5
VMEM = 127 * 2**19
ROW_GROUPS = 2
SIDE_GROUPS = 2
BF, F32 = jnp.bfloat16, jnp.float32
LOG_ROWS = 16
TERMS = 3


def pipelined(units, finish):
    def scores(unit):
        return lax.dot_general(
            unit[0](), unit[1], (((1,), (1,)), ((), ())), preferred_element_type=F32
        )

    coming = scores(units[0])
    for number, unit in enumerate(units):
        s = coming
        if number + 1 < len(units):
            coming = scores(units[number + 1])
        peak = jnp.max(s, axis=1, keepdims=True)
        weights = jnp.exp2((s - peak) * SCALE2)
        total = jnp.sum(weights, axis=1, keepdims=True)
        summed = jnp.dot(weights.astype(BF), unit[2], preferred_element_type=F32)
        finish(number, summed / total, peak * SCALE2 + jnp.log2(total))


def one_hot(c, transposed_rows):
    row = lax.broadcasted_iota(jnp.int32, (LOG_ROWS, HD), 0) - c * TERMS
    lane = lax.broadcasted_iota(jnp.int32, (LOG_ROWS, HD), 1)
    hit = (row >= 0) & (row < TERMS) if transposed_rows else (row == lane) & (row >= 0) & (row < TERMS)
    return jnp.where(hit, 1.0, 0.0).astype(BF)


def write_logs(ref, cols, log):
    lane = lax.broadcasted_iota(jnp.int32, (TILE, HD), 1)
    first = log.astype(BF).astype(F32)
    second = (log - first).astype(BF).astype(F32)
    terms = jnp.where(lane == 0, first, jnp.where(lane == 1, second, log - first - second)).astype(BF)
    block = functools.reduce(
        jnp.add,
        [
            lax.dot_general(
                one_hot(c, False), terms[c * HD : (c + 1) * HD], (((1,), (1,)), ((), ())),
                preferred_element_type=F32,
            )
            for c in range(TILE // HD)
        ],
    )
    ref[TILE:, cols] = block.astype(ref.dtype)


def read_logs(ref, cols):
    block = ref[TILE:, cols].astype(BF)
    return jnp.concatenate(
        [
            lax.dot_general(
                block, one_hot(c, True), (((0,), (0,)), ((), ())), preferred_element_type=F32
            )
            for c in range(TILE // HD)
        ],
        axis=0,
    )


def lanes(i):
    return slice(i * HD, (i + 1) * HD)


def pass_flags(flags, token):
    for i in range(8):
        token[i] = flags[i]


def window_kernel(jobs, n_q, n_kv, n_after, split, heads, flags, *refs):
    refs = refs[n_after:]
    q_refs = refs[:n_q]
    kv_refs = refs[n_q : n_q + n_kv]
    outs = refs[n_q + n_kv : n_q + n_kv + len(jobs)]
    token, log_ref = refs[n_q + n_kv + len(jobs) :]
    pass_flags(flags, token)
    size = TILE // split
    units, where = [], []
    for head in range(heads):
        at = lanes(head)
        for number, (qi, kvs) in enumerate(jobs):
            keys = jnp.concatenate([kv_refs[i][t, 0, :, at] for i in kvs for t in range(TT)], axis=0)
            values = jnp.concatenate([kv_refs[i][t, 1, :, at] for i in kvs for t in range(TT)], axis=0)
            for part in range(split):
                cut = slice(part * size, (part + 1) * size)
                units.append((lambda qi=qi, cut=cut, at=at: q_refs[qi][cut, at], keys, values))
                where.append((number, cut, at, part))

    def finish(unit, out, log):
        number, cut, at, part = where[unit]
        outs[number][cut, at] = out.astype(outs[number].dtype)
        log = jnp.broadcast_to(log, (size, HD))
        if split > 1:
            log_ref[unit // split, cut, :] = log
            log = log_ref[unit // split]
        if part == split - 1:
            write_logs(outs[number], at, log)

    pipelined(units, finish)


def window(name, flags, qs, kvs, jobs, h0, nh, out_types, split, step, flops=1000, after=()):
    smem = pl.BlockSpec(memory_space=pltpu.SMEM)
    base = h0 // step
    specs = [smem] + [pl.BlockSpec(memory_space=pl.ANY) for _ in after]
    specs += [pl.BlockSpec((TILE, step * HD), lambda h: (0, h + base)) for _ in qs]
    specs += [pl.BlockSpec((TT, 2, TILE, step * HD), lambda h: (0, 0, 0, h + base)) for _ in kvs]
    rows = TILE + LOG_ROWS
    res = pl.pallas_call(
        functools.partial(window_kernel, jobs, len(qs), len(kvs), len(after), split, step),
        grid=(nh // step,),
        in_specs=specs,
        out_specs=[pl.BlockSpec((rows, step * HD), lambda h: (0, h)) for _ in jobs] + [smem],
        out_shape=[jax.ShapeDtypeStruct((rows, nh * HD), t) for t in out_types]
        + [jax.ShapeDtypeStruct(flags.shape, flags.dtype)],
        scratch_shapes=[pltpu.VMEM((len(jobs) * step, TILE, HD), F32)],
        compiler_params=pltpu.CompilerParams(vmem_limit_bytes=VMEM),
        cost_estimate=pl.CostEstimate(flops=flops, bytes_accessed=1000, transcendentals=0),
        name=name,
    )(flags, *after, *qs, *kvs)
    return res[-1], res[:-1]


def merge_parts(parts):
    top = functools.reduce(jnp.maximum, [p[1] for p in parts])
    scales = [jnp.exp2(p[1] - top) for p in parts]
    total = functools.reduce(jnp.add, scales)
    summed = functools.reduce(jnp.add, [p[0].astype(F32) * s for p, s in zip(parts, scales)])
    return summed, top, total


def merge_kernel(part_flags, heads, flags, *refs):
    n = len(part_flags)
    out, token = refs[n:]
    pass_flags(flags, token)
    for head in range(heads):
        at = lanes(head)
        parts = [
            (refs[i][:TILE, at], jnp.where(flags[f] != 0, read_logs(refs[i], at), NEG))
            for i, f in enumerate(part_flags)
        ]
        summed, top, total = merge_parts(parts)
        out[:TILE, at] = (summed / total).astype(out.dtype)
        write_logs(out, at, top + jnp.log2(total))


def merge(name, flags, parts, part_flags, nh, step):
    smem = pl.BlockSpec(memory_space=pltpu.SMEM)
    block = pl.BlockSpec((TILE + LOG_ROWS, step * HD), lambda h: (0, h))
    res = pl.pallas_call(
        functools.partial(merge_kernel, part_flags, step),
        grid=(nh // step,),
        in_specs=[smem] + [block] * len(parts),
        out_specs=[block, smem],
        out_shape=[
            jax.ShapeDtypeStruct((TILE + LOG_ROWS, nh * HD), BF),
            jax.ShapeDtypeStruct(flags.shape, flags.dtype),
        ],
        compiler_params=pltpu.CompilerParams(vmem_limit_bytes=VMEM),
        cost_estimate=pl.CostEstimate(flops=1000, bytes_accessed=1000, transcendentals=0),
        name=name,
    )(flags, *parts)
    return res[1], res[0]


def far_kernel(width, heads, flags, offsets, q_ref, tiles, out_ref, token, buffer, sems):
    step = pl.program_id(0)
    pass_flags(flags, token)

    def copy(i):
        owner = lax.rem(flags[6] + 1 + offsets[i], width)
        cols = pl.ds(pl.multiple_of(i // FAR * HD, HD), HD)
        return pltpu.make_async_copy(tiles.at[owner, :, :, cols], buffer.at[i], sems.at[i])

    @pl.when(step == 0)
    def _():
        @pl.loop(0, HEADS * FAR)
        def _(i):
            copy(i).start()

    for i in range(heads * FAR):
        copy(step * (heads * FAR) + i).wait()
    units = []
    for head in range(heads):
        first = (step * heads + head) * FAR
        units.append(
            (
                lambda head=head: q_ref[:, lanes(head)],
                jnp.concatenate([buffer[first + f, 0] for f in range(FAR)], axis=0),
                jnp.concatenate([buffer[first + f, 1] for f in range(FAR)], axis=0),
            )
        )

    def finish(head, out, log):
        out_ref[:TILE, lanes(head)] = out
        write_logs(out_ref, lanes(head), jnp.broadcast_to(log, (TILE, HD)))

    pipelined(units, finish)


def far(flags, offsets, q, tiles, step):
    smem = pl.BlockSpec(memory_space=pltpu.SMEM)
    res = pl.pallas_call(
        functools.partial(far_kernel, tiles.shape[0], step),
        grid=(HEADS // step,),
        in_specs=[
            smem, smem, pl.BlockSpec((TILE, step * HD), lambda h: (0, h)), pl.BlockSpec(memory_space=pl.ANY)
        ],
        out_specs=[pl.BlockSpec((TILE + LOG_ROWS, step * HD), lambda h: (0, h)), smem],
        out_shape=[
            jax.ShapeDtypeStruct((TILE + LOG_ROWS, HEADS * HD), F32),
            jax.ShapeDtypeStruct(flags.shape, flags.dtype),
        ],
        scratch_shapes=[
            pltpu.VMEM((HEADS * FAR, 2, TILE, HD), BF),
            pltpu.SemaphoreType.DMA((HEADS * FAR,)),
        ],
        compiler_params=pltpu.CompilerParams(vmem_limit_bytes=VMEM),
        cost_estimate=pl.CostEstimate(flops=1000, bytes_accessed=1000, transcendentals=0),
        name="far",
    )(flags, offsets, q, tiles)
    return res[1], res[0]


def final_kernel(part_specs, heads, flags, *refs):
    arrays, out_ref = refs[:-1], refs[-1]
    step = pl.program_id(0)
    for head in range(heads):
        at = lanes(head)
        parts, place = [], 0
        for flag, groups in part_specs:
            per = HEADS // groups // heads
            sums, log = arrays[place][:TILE, at].astype(F32), read_logs(arrays[place], at)
            for g in range(1, groups):
                later = step >= g * per
                sums = jnp.where(later, arrays[place + g][:TILE, at].astype(F32), sums)
                log = jnp.where(later, read_logs(arrays[place + g], at), log)
            place += groups
            parts.append((sums, jnp.where(flags[flag] != 0, log, NEG)))
        merged, _, scale = merge_parts(parts)
        out_ref[:, at] = (merged / scale).astype(out_ref.dtype)


def final(flags, parts, step):
    specs, arrays = [], []
    for _, group_arrays in parts:
        per = HEADS // len(group_arrays) // step
        for g, array in enumerate(group_arrays):
            index = functools.partial(
                lambda h, low, top: (0, jnp.clip(h - low, 0, top)), low=g * per, top=per - 1
            )
            specs.append(pl.BlockSpec((TILE + LOG_ROWS, step * HD), index))
            arrays.append(array)
    return pl.pallas_call(
        functools.partial(final_kernel, [(f, len(a)) for f, a in parts], step),
        grid=(HEADS // step,),
        in_specs=[pl.BlockSpec(memory_space=pltpu.SMEM)] + specs,
        out_specs=pl.BlockSpec((TILE, step * HD), lambda h: (0, h)),
        out_shape=jax.ShapeDtypeStruct((TILE, HEADS * HD), BF),
        compiler_params=pltpu.CompilerParams(vmem_limit_bytes=VMEM),
        cost_estimate=pl.CostEstimate(flops=1000, bytes_accessed=1000, transcendentals=0),
        name="final",
    )(flags, *arrays)


def on_device(queries, keys_values, far_offsets):
    width, height = lax.axis_size("wa"), lax.axis_size("ha")
    col, row = lax.axis_index("wa"), lax.axis_index("ha")
    up = [(i, i + 1) for i in range(height - 1)]
    down = [(j, i) for i, j in up]
    mate = [(i, i ^ 1) for i in range(width)]
    across = [(i, i + 1) for i in range(1, width - 1, 2)]
    across = across + [(j, i) for i, j in across]

    q = queries.reshape(TILE, HEADS * HD)
    kv = keys_values.reshape(TT, 2, TILE, HEADS * HD)

    lo, hi = row > 0, row < height - 1
    side = (col > 0) & (col < width - 1)
    flags = jnp.stack(
        [jnp.int32(1)] + [f.astype(jnp.int32) for f in (lo, hi, side, side & lo, side & hi)] + [col, row]
    )

    q_side = lax.ppermute(q, "wa", across)
    q_lo = lax.ppermute(q, "ha", up)
    q_hi = lax.ppermute(q, "ha", down)
    kv_mate = lax.ppermute(kv, "wa", mate)

    flags, (own,) = window("own", flags, [q], [kv], [(0, (0,))], 0, HEADS, [F32], 2, 3)
    q_side, middle, flags = lax.optimization_barrier((q_side, kv[1], flags))
    qs_lo = lax.ppermute(q_side, "ha", up)
    qs_hi = lax.ppermute(q_side, "ha", down)
    tiles = lax.all_gather(middle, "wa")

    def rows(flags, name, q_there, flops=1000, after=()):
        flags, (o,) = window(
            name, flags, [q_there], [kv, kv_mate], [(0, (0, 1))], 0, HEADS, [BF], 2, 3, flops, after
        )
        return flags, o

    def side_part(flags, g):
        per = HEADS // SIDE_GROUPS
        flags, (s_lo, s_hi, s_own) = window(
            "side", flags, [qs_lo, qs_hi, q_side], [kv], [(0, (0,)), (1, (0,)), (2, (0,))],
            g * per, per, [BF, BF, F32], 1, 2,
        )
        return flags, [s_own, lax.ppermute(s_hi, "ha", up), lax.ppermute(s_lo, "ha", down)]

    flags, o_lo = rows(flags, "row_lo", q_lo, 10**13, [q_hi])
    from_hi = lax.ppermute(o_lo, "ha", down)
    pending, sides = [], []
    for g in range(SIDE_GROUPS):
        flags, parts = side_part(flags, g)
        pending.append(parts)
    flags, o_hi = rows(flags, "row_hi", q_hi)
    from_lo = lax.ppermute(o_hi, "ha", up)
    for parts in pending:
        flags, merged = merge("side_merge", flags, parts, [3, 4, 5], HEADS // SIDE_GROUPS, 6)
        sides.append(lax.ppermute(merged, "wa", across))
    flags, (mates,) = window("mate", flags, [q], [kv_mate], [(0, (0,))], 0, HEADS, [F32], 2, 3)
    flags, far_part = far(flags, far_offsets.reshape(-1), q, tiles, 4)
    out = final(
        flags,
        [(0, [own]), (0, [mates]), (0, [far_part]), (1, [from_lo]), (2, [from_hi]), (3, sides)],
        6,
    )
    return out.reshape(queries.shape)


def solution(mesh):
    placed = (
        P("ha", "wa", None, None),
        P("ha", "wa", None, None, None, None),
        P("wa", "ha", None, None),
    )
    return jax.shard_map(
        on_device, mesh=mesh, in_specs=placed, out_specs=P("ha", "wa", None, None), check_vma=False
    )
```

```python
import functools

import jax
import jax.numpy as jnp
from jax import lax
from jax.experimental import pallas as pl
from jax.experimental.pallas import tpu as pltpu
from jax.sharding import PartitionSpec as P

HEADS = 12
HD = 128
TILE = 384
TT = 3
FAR = 2
NEG = -1e30
SCALE2 = 1.4426950408889634 / HD**0.5
VMEM = 127 * 2**19
ROW_GROUPS = 2
SIDE_GROUPS = 2
BF, F32 = jnp.bfloat16, jnp.float32
LOG_ROWS = 16
BLOCK = HD + LOG_ROWS


SAMPLE = 128
LIMIT = 2.0**100


def attend(q, keys, values, peak):
    s = lax.dot_general(keys, q, (((1,), (1,)), ((), ())), preferred_element_type=F32)
    if peak is None:
        peak = jnp.max(s, axis=0, keepdims=True)
    weights = jnp.exp2((s - peak) * SCALE2)
    total = jnp.sum(weights, axis=0, keepdims=True)
    summed = jnp.dot(values, weights.astype(BF), preferred_element_type=F32)
    return summed, total, peak


def attend_all(heads, groups, get, finish):
    worst = None
    for head in range(heads):
        for group in range(groups):
            q, keys, values = get(head, group)
            some = lax.dot_general(
                keys[:SAMPLE], q, (((1,), (1,)), ((), ())), preferred_element_type=F32
            )
            peak = jnp.max(some, axis=0, keepdims=True)
            summed, total, _ = attend(q, keys, values, peak)
            finish(head, group, summed / total, peak * SCALE2 + jnp.log2(total))
            worst = total if worst is None else jnp.maximum(worst, total)

    @pl.when(jnp.logical_not(jnp.max(worst) < LIMIT))
    def _():
        @pl.loop(0, heads)
        def _(head):
            for group in range(groups):
                summed, total, peak = attend(*get(head, group), None)
                finish(head, group, summed / total, peak * SCALE2 + jnp.log2(total))


def rows_of(head, start, size):
    low = head * BLOCK + start
    return pl.ds(low if isinstance(head, int) else pl.multiple_of(low, 16), size)


def write_part(ref, head, out, log):
    first = log.astype(BF).astype(F32)
    second = (log - first).astype(BF).astype(F32)
    row = lax.broadcasted_iota(jnp.int32, (LOG_ROWS, log.shape[1]), 0)
    third = jnp.where(row == 2, log - first - second, 0.0)
    terms = jnp.where(row == 0, first, jnp.where(row == 1, second, third))
    ref[rows_of(head, 0, HD), :] = out.astype(ref.dtype)
    ref[rows_of(head, HD, LOG_ROWS), :] = terms.astype(ref.dtype)


def read_part(ref, head):
    low = head * BLOCK
    log = jnp.sum(ref[low + HD : low + BLOCK, :].astype(F32), axis=0, keepdims=True)
    return ref[low : low + HD, :].astype(F32), log


def lanes(i):
    return pl.ds(i * HD if isinstance(i, int) else pl.multiple_of(i * HD, HD), HD)


def pass_flags(flags, token):
    for i in range(8):
        token[i] = flags[i]


def window_kernel(jobs, n_q, n_kv, n_after, join, heads, flags, *refs):
    refs = refs[n_after:]
    q_refs = refs[:n_q]
    kv_refs = refs[n_q : n_q + n_kv]
    outs = refs[n_q + n_kv : n_q + n_kv + len(jobs)]
    pass_flags(flags, refs[n_q + n_kv + len(jobs)])
    groups = [list(range(i, min(i + join, len(jobs)))) for i in range(0, len(jobs), join)]

    def get(head, group):
        at = lanes(head)
        kvs = [kv_refs[i] for i in jobs[groups[group][0]][1]]
        q = jnp.concatenate([q_refs[jobs[j][0]][:, at] for j in groups[group]], axis=0)
        keys = jnp.concatenate([kv[t, 0, :, at] for kv in kvs for t in range(TT)], axis=0)
        values = jnp.concatenate([kv[t, 1, :, at].T for kv in kvs for t in range(TT)], axis=1)
        return q, keys, values

    def finish(head, group, out, log):
        for k, j in enumerate(groups[group]):
            cut = slice(k * TILE, (k + 1) * TILE)
            write_part(outs[j], head, out[:, cut], log[:, cut])

    attend_all(heads, len(groups), get, finish)


def window(name, flags, qs, kvs, jobs, h0, nh, out_types, join, step, flops=1000, after=()):
    smem = pl.BlockSpec(memory_space=pltpu.SMEM)
    base = h0 // step
    specs = [smem] + [pl.BlockSpec(memory_space=pl.ANY) for _ in after]
    specs += [pl.BlockSpec((TILE, step * HD), lambda h: (0, h + base)) for _ in qs]
    specs += [pl.BlockSpec((TT, 2, TILE, step * HD), lambda h: (0, 0, 0, h + base)) for _ in kvs]
    res = pl.pallas_call(
        functools.partial(window_kernel, jobs, len(qs), len(kvs), len(after), join, step),
        grid=(nh // step,),
        in_specs=specs,
        out_specs=[pl.BlockSpec((step * BLOCK, TILE), lambda h: (h, 0)) for _ in jobs] + [smem],
        out_shape=[jax.ShapeDtypeStruct((nh * BLOCK, TILE), t) for t in out_types]
        + [jax.ShapeDtypeStruct(flags.shape, flags.dtype)],
        compiler_params=pltpu.CompilerParams(vmem_limit_bytes=VMEM),
        cost_estimate=pl.CostEstimate(flops=flops, bytes_accessed=1000, transcendentals=0),
        name=name,
    )(flags, *after, *qs, *kvs)
    return res[-1], res[:-1]


def merge_parts(parts):
    top = functools.reduce(jnp.maximum, [p[1] for p in parts])
    scales = [jnp.exp2(p[1] - top) for p in parts]
    total = functools.reduce(jnp.add, scales)
    out = functools.reduce(jnp.add, [p[0] * (s / total) for p, s in zip(parts, scales)])
    return out, top + jnp.log2(total)


def masked(part, flag):
    return part[0], jnp.where(flag != 0, part[1], NEG)


def merge_kernel(part_flags, n_after, heads, flags, *refs):
    refs = refs[n_after:]
    n = len(part_flags)
    out, token = refs[n:]
    pass_flags(flags, token)
    for head in range(heads):
        write_part(
            out, head, *merge_parts([masked(read_part(refs[i], head), flags[f]) for i, f in enumerate(part_flags)])
        )


def merge(name, flags, parts, part_flags, nh, step, after=()):
    smem = pl.BlockSpec(memory_space=pltpu.SMEM)
    block = pl.BlockSpec((step * BLOCK, TILE), lambda h: (h, 0))
    res = pl.pallas_call(
        functools.partial(merge_kernel, part_flags, len(after), step),
        grid=(nh // step,),
        in_specs=[smem] + [pl.BlockSpec(memory_space=pl.ANY)] * len(after) + [block] * len(parts),
        out_specs=[block, smem],
        out_shape=[
            jax.ShapeDtypeStruct((nh * BLOCK, TILE), BF),
            jax.ShapeDtypeStruct(flags.shape, flags.dtype),
        ],
        compiler_params=pltpu.CompilerParams(vmem_limit_bytes=VMEM),
        cost_estimate=pl.CostEstimate(flops=1000, bytes_accessed=1000, transcendentals=0),
        name=name,
    )(flags, *after, *parts)
    return res[1], res[0]


def far_kernel(width, heads, flags, offsets, q_ref, tiles, _, out_ref, token, buffer, sems):
    step = pl.program_id(0)
    pass_flags(flags, token)

    def copy(i):
        owner = lax.rem(flags[6] + 1 + offsets[i], width)
        cols = pl.ds(pl.multiple_of(i // FAR * HD, HD), HD)
        return pltpu.make_async_copy(tiles.at[owner, :, :, cols], buffer.at[i], sems.at[i])

    @pl.when(step == 0)
    def _():
        @pl.loop(0, HEADS * FAR)
        def _(i):
            copy(i).start()

    for i in range(heads * FAR):
        copy(step * (heads * FAR) + i).wait()

    def get(head, _):
        first = (step * heads + head) * FAR
        keys = jnp.concatenate([buffer[first + f, 0] for f in range(FAR)], axis=0)
        values = jnp.concatenate([buffer[first + f, 1].T for f in range(FAR)], axis=1)
        return q_ref[:, lanes(head)], keys, values

    attend_all(heads, 1, get, lambda head, _, out, log: write_part(out_ref, head, out, log))


def far(flags, offsets, q, tiles, step, after):
    smem = pl.BlockSpec(memory_space=pltpu.SMEM)
    res = pl.pallas_call(
        functools.partial(far_kernel, tiles.shape[0], step),
        grid=(HEADS // step,),
        in_specs=[
            smem, smem, pl.BlockSpec((TILE, step * HD), lambda h: (0, h))
        ] + [pl.BlockSpec(memory_space=pl.ANY)] * 2,
        out_specs=[pl.BlockSpec((step * BLOCK, TILE), lambda h: (h, 0)), smem],
        out_shape=[
            jax.ShapeDtypeStruct((HEADS * BLOCK, TILE), F32),
            jax.ShapeDtypeStruct(flags.shape, flags.dtype),
        ],
        scratch_shapes=[
            pltpu.VMEM((HEADS * FAR, 2, TILE, HD), BF),
            pltpu.SemaphoreType.DMA((HEADS * FAR,)),
        ],
        compiler_params=pltpu.CompilerParams(vmem_limit_bytes=VMEM),
        cost_estimate=pl.CostEstimate(flops=10**13, bytes_accessed=1000, transcendentals=0),
        name="far",
    )(flags, offsets, q, tiles, after)
    return res[1], res[0]


def final_kernel(part_specs, heads, flags, *refs):
    arrays, out_ref = refs[:-1], refs[-1]
    step = pl.program_id(0)
    for head in range(heads):
        parts, place = [], 0
        for flag, groups in part_specs:
            per = HEADS // groups // heads
            part = read_part(arrays[place], head)
            for g in range(1, groups):
                later = read_part(arrays[place + g], head)
                part = tuple(jnp.where(step >= g * per, a, b) for a, b in zip(later, part))
            place += groups
            parts.append(masked(part, flags[flag]))
        out_ref[:, lanes(head)] = merge_parts(parts)[0].T.astype(out_ref.dtype)


def final(flags, parts, step):
    specs, arrays = [], []
    for _, group_arrays in parts:
        per = HEADS // len(group_arrays) // step
        for g, array in enumerate(group_arrays):
            index = functools.partial(
                lambda h, low, top: (jnp.clip(h - low, 0, top), 0), low=g * per, top=per - 1
            )
            specs.append(pl.BlockSpec((step * BLOCK, TILE), index))
            arrays.append(array)
    return pl.pallas_call(
        functools.partial(final_kernel, [(f, len(a)) for f, a in parts], step),
        grid=(HEADS // step,),
        in_specs=[pl.BlockSpec(memory_space=pltpu.SMEM)] + specs,
        out_specs=pl.BlockSpec((TILE, step * HD), lambda h: (0, h)),
        out_shape=jax.ShapeDtypeStruct((TILE, HEADS * HD), BF),
        compiler_params=pltpu.CompilerParams(vmem_limit_bytes=VMEM),
        cost_estimate=pl.CostEstimate(flops=1000, bytes_accessed=1000, transcendentals=0),
        name="final",
    )(flags, *arrays)


def on_device(queries, keys_values, far_offsets):
    width, height = lax.axis_size("wa"), lax.axis_size("ha")
    col, row = lax.axis_index("wa"), lax.axis_index("ha")
    up = [(i, i + 1) for i in range(height - 1)]
    down = [(j, i) for i, j in up]
    mate = [(i, i ^ 1) for i in range(width)]
    across = [(i, i + 1) for i in range(1, width - 1, 2)]
    across = across + [(j, i) for i, j in across]

    q = queries.reshape(TILE, HEADS * HD)
    kv = keys_values.reshape(TT, 2, TILE, HEADS * HD)

    lo, hi = row > 0, row < height - 1
    side = (col > 0) & (col < width - 1)
    flags = jnp.stack(
        [jnp.int32(1)] + [f.astype(jnp.int32) for f in (lo, hi, side, side & lo, side & hi)] + [col, row]
    )

    kv_mate = lax.ppermute(kv, "wa", mate)
    q_side = lax.ppermute(q, "wa", across)
    q_lo = lax.ppermute(q, "ha", up)
    q_hi = lax.ppermute(q, "ha", down)
    middle = kv[1]

    flags, (own,) = window("own", flags, [q], [kv, kv_mate], [(0, (0, 1))], 0, HEADS, [F32], 1, 3, after=[middle])
    tiles = lax.all_gather(middle, "wa")
    q_side, flags = lax.optimization_barrier((q_side, flags))
    qs_lo = lax.ppermute(q_side, "ha", up)
    qs_hi = lax.ppermute(q_side, "ha", down)

    def side_part(flags, g, flops):
        per = HEADS // SIDE_GROUPS
        flags, (s_lo, s_hi, s_own) = window(
            "side", flags, [qs_lo, qs_hi, q_side], [kv], [(0, (0,)), (1, (0,)), (2, (0,))],
            g * per, per, [BF, BF, F32], 3, 2, flops,
        )
        return flags, [s_own, lax.ppermute(s_hi, "ha", up), lax.ppermute(s_lo, "ha", down)]

    def side_return(flags, parts, after):
        flags, merged = merge("side_merge", flags, parts, [3, 4, 5], HEADS // SIDE_GROUPS, 6, after)
        return flags, lax.ppermute(merged, "wa", across)

    flags, (o_lo, o_hi) = window(
        "rows", flags, [q_lo, q_hi], [kv, kv_mate], [(0, (0, 1)), (1, (0, 1))], 0, HEADS, [BF, BF], 2, 2, 10**13
    )
    from_lo = lax.ppermute(o_hi, "ha", up)
    from_hi = lax.ppermute(o_lo, "ha", down)
    flags, first = side_part(flags, 0, 2 * 10**10)
    flags, second = side_part(flags, 1, 1000)
    flags, first = side_return(flags, first, [from_lo, from_hi])
    flags, second = side_return(flags, second, [])
    flags, far_part = far(flags, far_offsets.reshape(-1), q, tiles, 3, first)
    out = final(
        flags, [(0, [own]), (0, [far_part]), (1, [from_lo]), (2, [from_hi]), (3, [first, second])], 6
    )
    return out.reshape(queries.shape)


def solution(mesh):
    placed = (
        P("ha", "wa", None, None),
        P("ha", "wa", None, None, None, None),
        P("wa", "ha", None, None),
    )
    return jax.shard_map(
        on_device, mesh=mesh, in_specs=placed, out_specs=P("ha", "wa", None, None), check_vma=False
    )
```

```python
import functools

import jax
import jax.numpy as jnp
from jax import lax
from jax.experimental import pallas as pl
from jax.experimental.pallas import tpu as pltpu
from jax.sharding import PartitionSpec as P

HEADS = 12
HD = 128
TILE = 384
TT = 3
FAR = 2
NEG = -1e30
SCALE2 = 1.4426950408889634 / HD**0.5
VMEM = 127 * 2**19
ROW_GROUPS = 2
SIDE_GROUPS = 2
BF, F32 = jnp.bfloat16, jnp.float32
LOG_ROWS = 16
BLOCK = HD + LOG_ROWS


SAMPLE = 128
LIMIT = 2.0**100


def attend(q, keys, values, peak):
    s = lax.dot_general(keys, q, (((1,), (1,)), ((), ())), preferred_element_type=F32)
    if peak is None:
        peak = jnp.max(s, axis=0, keepdims=True)
    weights = jnp.exp2((s - peak) * SCALE2)
    total = jnp.sum(weights, axis=0, keepdims=True)
    summed = jnp.dot(values, weights.astype(BF), preferred_element_type=F32)
    return summed, total, peak


def attend_all(heads, groups, get, finish):
    worst = None
    for head in range(heads):
        for group in range(groups):
            q, keys, values = get(head, group)
            some = lax.dot_general(
                keys[:SAMPLE], q, (((1,), (1,)), ((), ())), preferred_element_type=F32
            )
            peak = jnp.max(some, axis=0, keepdims=True)
            summed, total, _ = attend(q, keys, values, peak)
            finish(head, group, summed / total, peak * SCALE2 + jnp.log2(total))
            worst = total if worst is None else jnp.maximum(worst, total)

    @pl.when(jnp.logical_not(jnp.max(worst) < LIMIT))
    def _():
        @pl.loop(0, heads)
        def _(head):
            for group in range(groups):
                summed, total, peak = attend(*get(head, group), None)
                finish(head, group, summed / total, peak * SCALE2 + jnp.log2(total))


def rows_of(head, start, size):
    low = head * BLOCK + start
    return pl.ds(low if isinstance(head, int) else pl.multiple_of(low, 16), size)


def write_part(ref, head, out, log):
    first = log.astype(BF).astype(F32)
    second = (log - first).astype(BF).astype(F32)
    row = lax.broadcasted_iota(jnp.int32, (LOG_ROWS, log.shape[1]), 0)
    third = jnp.where(row == 2, log - first - second, 0.0)
    terms = jnp.where(row == 0, first, jnp.where(row == 1, second, third))
    ref[rows_of(head, 0, HD), :] = out.astype(ref.dtype)
    ref[rows_of(head, HD, LOG_ROWS), :] = terms.astype(ref.dtype)


def read_part(ref, head):
    low = head * BLOCK
    log = jnp.sum(ref[low + HD : low + BLOCK, :].astype(F32), axis=0, keepdims=True)
    return ref[low : low + HD, :].astype(F32), log


def lanes(i):
    return pl.ds(i * HD if isinstance(i, int) else pl.multiple_of(i * HD, HD), HD)


def pass_flags(flags, token):
    for i in range(8):
        token[i] = flags[i]


def window_kernel(jobs, n_q, n_kv, n_after, join, heads, flags, *refs):
    refs = refs[n_after:]
    q_refs = refs[:n_q]
    kv_refs = refs[n_q : n_q + n_kv]
    outs = refs[n_q + n_kv : n_q + n_kv + len(jobs)]
    pass_flags(flags, refs[n_q + n_kv + len(jobs)])
    groups = [list(range(i, min(i + join, len(jobs)))) for i in range(0, len(jobs), join)]

    def get(head, group):
        at = lanes(head)
        kvs = [kv_refs[i] for i in jobs[groups[group][0]][1]]
        q = jnp.concatenate([q_refs[jobs[j][0]][:, at] for j in groups[group]], axis=0)
        keys = jnp.concatenate([kv[t, 0, :, at] for kv in kvs for t in range(TT)], axis=0)
        values = jnp.concatenate([kv[t, 1, :, at].T for kv in kvs for t in range(TT)], axis=1)
        return q, keys, values

    def finish(head, group, out, log):
        for k, j in enumerate(groups[group]):
            cut = slice(k * TILE, (k + 1) * TILE)
            write_part(outs[j], head, out[:, cut], log[:, cut])

    attend_all(heads, len(groups), get, finish)


def window(name, flags, qs, kvs, jobs, h0, nh, out_types, join, step, flops=1000, after=()):
    smem = pl.BlockSpec(memory_space=pltpu.SMEM)
    base = h0 // step
    specs = [smem] + [pl.BlockSpec(memory_space=pl.ANY) for _ in after]
    specs += [pl.BlockSpec((TILE, step * HD), lambda h: (0, h + base)) for _ in qs]
    specs += [pl.BlockSpec((TT, 2, TILE, step * HD), lambda h: (0, 0, 0, h + base)) for _ in kvs]
    res = pl.pallas_call(
        functools.partial(window_kernel, jobs, len(qs), len(kvs), len(after), join, step),
        grid=(nh // step,),
        in_specs=specs,
        out_specs=[pl.BlockSpec((step * BLOCK, TILE), lambda h: (h, 0)) for _ in jobs] + [smem],
        out_shape=[jax.ShapeDtypeStruct((nh * BLOCK, TILE), t) for t in out_types]
        + [jax.ShapeDtypeStruct(flags.shape, flags.dtype)],
        compiler_params=pltpu.CompilerParams(vmem_limit_bytes=VMEM),
        cost_estimate=pl.CostEstimate(flops=flops, bytes_accessed=1000, transcendentals=0),
        name=name,
    )(flags, *after, *qs, *kvs)
    return res[-1], res[:-1]


def merge_parts(parts):
    top = functools.reduce(jnp.maximum, [p[1] for p in parts])
    scales = [jnp.exp2(p[1] - top) for p in parts]
    total = functools.reduce(jnp.add, scales)
    out = functools.reduce(jnp.add, [p[0] * (s / total) for p, s in zip(parts, scales)])
    return out, top + jnp.log2(total)


def masked(part, flag):
    return part[0], jnp.where(flag != 0, part[1], NEG)


def merge_kernel(part_flags, n_after, heads, flags, *refs):
    refs = refs[n_after:]
    n = len(part_flags)
    out, token = refs[n:]
    pass_flags(flags, token)
    for head in range(heads):
        write_part(
            out, head, *merge_parts([masked(read_part(refs[i], head), flags[f]) for i, f in enumerate(part_flags)])
        )


def merge(name, flags, own, h0, parts, part_flags, nh, step, flops, after):
    smem = pl.BlockSpec(memory_space=pltpu.SMEM)
    block = pl.BlockSpec((step * BLOCK, TILE), lambda h: (h, 0))
    res = pl.pallas_call(
        functools.partial(merge_kernel, part_flags, len(after), step),
        grid=(nh // step,),
        in_specs=[smem] + [pl.BlockSpec(memory_space=pl.ANY)] * len(after)
        + [pl.BlockSpec((step * BLOCK, TILE), lambda h: (h + h0 // step, 0))]
        + [block] * len(parts),
        out_specs=[block, smem],
        out_shape=[
            jax.ShapeDtypeStruct((nh * BLOCK, TILE), BF),
            jax.ShapeDtypeStruct(flags.shape, flags.dtype),
        ],
        compiler_params=pltpu.CompilerParams(vmem_limit_bytes=VMEM),
        cost_estimate=pl.CostEstimate(flops=flops, bytes_accessed=1000, transcendentals=0),
        name=name,
    )(flags, *after, own, *parts)
    return res[1], res[0]


def far_kernel(width, h0, nh, heads, flags, offsets, q_ref, tiles, *refs):
    out_ref, token, buffer, sems = refs[-4:]
    step = pl.program_id(0)
    pass_flags(flags, token)

    def copy(i):
        owner = lax.rem(flags[6] + 1 + offsets[h0 * FAR + i], width)
        cols = pl.ds(pl.multiple_of(h0 * HD + i // FAR * HD, HD), HD)
        return pltpu.make_async_copy(tiles.at[owner, :, :, cols], buffer.at[i], sems.at[i])

    @pl.when(step == 0)
    def _():
        @pl.loop(0, nh * FAR)
        def _(i):
            copy(i).start()

    for i in range(heads * FAR):
        copy(step * (heads * FAR) + i).wait()

    def get(head, _):
        first = (step * heads + head) * FAR
        keys = jnp.concatenate([buffer[first + f, 0] for f in range(FAR)], axis=0)
        values = jnp.concatenate([buffer[first + f, 1].T for f in range(FAR)], axis=1)
        return q_ref[:, lanes(head)], keys, values

    attend_all(heads, 1, get, lambda head, _, out, log: write_part(out_ref, head, out, log))


def far(flags, offsets, q, tiles, h0, nh, step, flops, after):
    smem = pl.BlockSpec(memory_space=pltpu.SMEM)
    res = pl.pallas_call(
        functools.partial(far_kernel, tiles.shape[0], h0, nh, step),
        grid=(nh // step,),
        in_specs=[
            smem, smem, pl.BlockSpec((TILE, step * HD), lambda h: (0, h + h0 // step))
        ] + [pl.BlockSpec(memory_space=pl.ANY)] * (1 + len(after)),
        out_specs=[pl.BlockSpec((step * BLOCK, TILE), lambda h: (h, 0)), smem],
        out_shape=[
            jax.ShapeDtypeStruct((nh * BLOCK, TILE), F32),
            jax.ShapeDtypeStruct(flags.shape, flags.dtype),
        ],
        scratch_shapes=[
            pltpu.VMEM((nh * FAR, 2, TILE, HD), BF),
            pltpu.SemaphoreType.DMA((nh * FAR,)),
        ],
        compiler_params=pltpu.CompilerParams(vmem_limit_bytes=VMEM),
        cost_estimate=pl.CostEstimate(flops=flops, bytes_accessed=1000, transcendentals=0),
        name="far",
    )(flags, offsets, q, tiles, *after)
    return res[1], res[0]


def final_kernel(part_flags, heads, flags, *refs):
    n = len(part_flags)
    arrays, out_ref, token = refs[:n], refs[-2], refs[-1]
    pass_flags(flags, token)
    for head in range(heads):
        parts = [masked(read_part(a, head), flags[f]) for a, f in zip(arrays, part_flags)]
        out_ref[:, lanes(head)] = merge_parts(parts)[0].T.astype(out_ref.dtype)


def final(flags, parts, h0, nh, step, out):
    smem = pl.BlockSpec(memory_space=pltpu.SMEM)
    specs = [
        pl.BlockSpec((step * BLOCK, TILE), functools.partial(lambda h, d: (h + d, 0), d=(h0 - base) // step))
        for _, base, _ in parts
    ]
    before = [] if out is None else [out]
    return pl.pallas_call(
        functools.partial(final_kernel, [f for f, _, _ in parts], step),
        grid=(nh // step,),
        in_specs=[smem] + specs + [pl.BlockSpec(memory_space=pl.ANY)] * len(before),
        out_specs=[pl.BlockSpec((TILE, step * HD), lambda h: (0, h + h0 // step)), smem],
        out_shape=[
            jax.ShapeDtypeStruct((TILE, HEADS * HD), BF),
            jax.ShapeDtypeStruct(flags.shape, flags.dtype),
        ],
        input_output_aliases={} if out is None else {1 + len(parts): 0},
        compiler_params=pltpu.CompilerParams(vmem_limit_bytes=VMEM),
        cost_estimate=pl.CostEstimate(flops=1000, bytes_accessed=1000, transcendentals=0),
        name="final",
    )(flags, *[a for _, _, a in parts], *before)


def on_device(queries, keys_values, far_offsets):
    width, height = lax.axis_size("wa"), lax.axis_size("ha")
    col, row = lax.axis_index("wa"), lax.axis_index("ha")
    up = [(i, i + 1) for i in range(height - 1)]
    down = [(j, i) for i, j in up]
    mate = [(i, i ^ 1) for i in range(width)]
    across = [(i, i + 1) for i in range(1, width - 1, 2)]
    across = across + [(j, i) for i, j in across]

    q = queries.reshape(TILE, HEADS * HD)
    kv = keys_values.reshape(TT, 2, TILE, HEADS * HD)

    lo, hi = row > 0, row < height - 1
    side = (col > 0) & (col < width - 1)
    flags = jnp.stack(
        [jnp.int32(1)] + [f.astype(jnp.int32) for f in (lo, hi, side, side & lo, side & hi)] + [col, row]
    )

    kv_mate = lax.ppermute(kv, "wa", mate)
    q_side = lax.ppermute(q, "wa", across)
    q_lo = lax.ppermute(q, "ha", up)
    q_hi = lax.ppermute(q, "ha", down)
    middle = kv[1]

    flags, (own,) = window("own", flags, [q], [kv, kv_mate], [(0, (0, 1))], 0, HEADS, [F32], 1, 3, after=[middle])
    tiles = lax.all_gather(middle, "wa")
    q_side, flags = lax.optimization_barrier((q_side, flags))
    qs_lo = lax.ppermute(q_side, "ha", up)
    qs_hi = lax.ppermute(q_side, "ha", down)

    per = HEADS // SIDE_GROUPS

    def side_rows(flags, g, flops):
        flags, (s_lo, s_hi) = window(
            "side_rows", flags, [qs_lo, qs_hi], [kv], [(0, (0,)), (1, (0,))], g * per, per, [BF, BF], 2, 2, flops
        )
        return flags, [lax.ppermute(s_hi, "ha", up), lax.ppermute(s_lo, "ha", down)]

    def side_return(flags, g, parts, flops, after):
        flags, merged = merge("side_merge", flags, s_own, g * per, parts, [3, 4, 5], per, 6, flops, after)
        return flags, lax.ppermute(merged, "wa", across)

    flags, (o_lo, o_hi) = window(
        "rows", flags, [q_lo, q_hi], [kv, kv_mate], [(0, (0, 1)), (1, (0, 1))], 0, HEADS, [BF, BF], 2, 2, 10**13
    )
    from_lo = lax.ppermute(o_hi, "ha", up)
    from_hi = lax.ppermute(o_lo, "ha", down)
    flags, first = side_rows(flags, 0, 2 * 10**10)
    flags, second = side_rows(flags, 1, 1000)
    flags, (s_own,) = window("side_own", flags, [q_side], [kv], [(0, (0,))], 0, HEADS, [F32], 1, 3)
    flags, first = side_return(flags, 0, first, 1000, [from_lo, from_hi])
    flags, second = side_return(flags, 1, second, 3 * 10**10, [])
    offsets = far_offsets.reshape(-1)
    flags, far_first = far(flags, offsets, q, tiles, 0, per, 3, 1000, [])
    flags, far_second = far(flags, offsets, q, tiles, per, per, 3, 10**13, [first])
    out = None
    for g, (side_merged, far_part) in enumerate([(first, far_first), (second, far_second)]):
        low = g * per
        out, flags = final(
            flags,
            [(0, 0, own), (0, low, far_part), (1, 0, from_lo), (2, 0, from_hi), (3, low, side_merged)],
            low, per, 3, out,
        )
    return out.reshape(queries.shape)


def solution(mesh):
    placed = (
        P("ha", "wa", None, None),
        P("ha", "wa", None, None, None, None),
        P("wa", "ha", None, None),
    )
    return jax.shard_map(
        on_device, mesh=mesh, in_specs=placed, out_specs=P("ha", "wa", None, None), check_vma=False
    )
```

```python
import functools

import jax
import jax.numpy as jnp
from jax import lax
from jax.experimental import pallas as pl
from jax.experimental.pallas import tpu as pltpu
from jax.sharding import PartitionSpec as P

HEADS = 12
HD = 128
TILE = 384
TT = 3
FAR = 2
NEG = -1e30
SCALE2 = 1.4426950408889634 / HD**0.5
VMEM = 127 * 2**19
GROUPS = ((0, 6), (6, 6))
BF, F32 = jnp.bfloat16, jnp.float32
LOG_ROWS = 16
BLOCK = HD + LOG_ROWS


SAMPLE = 128
LIMIT = 2.0**100


def attend(q, keys, values, peak):
    s = lax.dot_general(keys, q, (((1,), (1,)), ((), ())), preferred_element_type=F32)
    if peak is None:
        peak = jnp.max(s, axis=0, keepdims=True)
    weights = jnp.exp2((s - peak) * SCALE2)
    total = jnp.sum(weights, axis=0, keepdims=True)
    summed = jnp.dot(values, weights.astype(BF), preferred_element_type=F32)
    return summed, total, peak


def attend_all(heads, groups, get, finish):
    worst = None
    for head in range(heads):
        for group in range(groups):
            q, keys, values = get(head, group)
            some = lax.dot_general(
                keys[:SAMPLE], q, (((1,), (1,)), ((), ())), preferred_element_type=F32
            )
            peak = jnp.max(some, axis=0, keepdims=True)
            summed, total, _ = attend(q, keys, values, peak)
            finish(head, group, summed / total, peak * SCALE2 + jnp.log2(total))
            worst = total if worst is None else jnp.maximum(worst, total)

    @pl.when(jnp.logical_not(jnp.max(worst) < LIMIT))
    def _():
        @pl.loop(0, heads)
        def _(head):
            for group in range(groups):
                summed, total, peak = attend(*get(head, group), None)
                finish(head, group, summed / total, peak * SCALE2 + jnp.log2(total))


def rows_of(head, start, size):
    low = head * BLOCK + start
    return pl.ds(low if isinstance(head, int) else pl.multiple_of(low, 16), size)


def write_part(ref, head, out, log):
    first = log.astype(BF).astype(F32)
    second = (log - first).astype(BF).astype(F32)
    row = lax.broadcasted_iota(jnp.int32, (LOG_ROWS, log.shape[1]), 0)
    third = jnp.where(row == 2, log - first - second, 0.0)
    terms = jnp.where(row == 0, first, jnp.where(row == 1, second, third))
    ref[rows_of(head, 0, HD), :] = out.astype(ref.dtype)
    ref[rows_of(head, HD, LOG_ROWS), :] = terms.astype(ref.dtype)


def read_part(ref, head):
    log = jnp.sum(ref[rows_of(head, HD, LOG_ROWS), :].astype(F32), axis=0, keepdims=True)
    return ref[rows_of(head, 0, HD), :].astype(F32), log


def lanes(i):
    return pl.ds(i * HD if isinstance(i, int) else pl.multiple_of(i * HD, HD), HD)


def pass_flags(flags, token):
    for i in range(8):
        token[i] = flags[i]


def window_kernel(jobs, n_q, n_kv, n_after, join, heads, flags, *refs):
    refs = refs[n_after:]
    q_refs = refs[:n_q]
    kv_refs = refs[n_q : n_q + n_kv]
    outs = refs[n_q + n_kv : n_q + n_kv + len(jobs)]
    pass_flags(flags, refs[n_q + n_kv + len(jobs)])
    groups = [list(range(i, min(i + join, len(jobs)))) for i in range(0, len(jobs), join)]

    def get(head, group):
        at = lanes(head)
        kvs = [kv_refs[i] for i in jobs[groups[group][0]][1]]
        q = jnp.concatenate([q_refs[jobs[j][0]][:, at] for j in groups[group]], axis=0)
        keys = jnp.concatenate([kv[t, 0, :, at] for kv in kvs for t in range(TT)], axis=0)
        values = jnp.concatenate([kv[t, 1, :, at].T for kv in kvs for t in range(TT)], axis=1)
        return q, keys, values

    def finish(head, group, out, log):
        for k, j in enumerate(groups[group]):
            cut = slice(k * TILE, (k + 1) * TILE)
            write_part(outs[j], head, out[:, cut], log[:, cut])

    attend_all(heads, len(groups), get, finish)


def window(name, flags, qs, kvs, jobs, h0, nh, out_types, join, step, flops=1000, after=()):
    smem = pl.BlockSpec(memory_space=pltpu.SMEM)
    base = h0 // step
    specs = [smem] + [pl.BlockSpec(memory_space=pl.ANY) for _ in after]
    specs += [pl.BlockSpec((TILE, step * HD), lambda h: (0, h + base)) for _ in qs]
    specs += [pl.BlockSpec((TT, 2, TILE, step * HD), lambda h: (0, 0, 0, h + base)) for _ in kvs]
    res = pl.pallas_call(
        functools.partial(window_kernel, jobs, len(qs), len(kvs), len(after), join, step),
        grid=(nh // step,),
        in_specs=specs,
        out_specs=[pl.BlockSpec((step * BLOCK, TILE), lambda h: (h, 0)) for _ in jobs] + [smem],
        out_shape=[jax.ShapeDtypeStruct((nh * BLOCK, TILE), t) for t in out_types]
        + [jax.ShapeDtypeStruct(flags.shape, flags.dtype)],
        compiler_params=pltpu.CompilerParams(vmem_limit_bytes=VMEM),
        cost_estimate=pl.CostEstimate(flops=flops, bytes_accessed=1000, transcendentals=0),
        name=name,
    )(flags, *after, *qs, *kvs)
    return res[-1], res[:-1]


def merge_parts(parts):
    top = functools.reduce(jnp.maximum, [p[1] for p in parts])
    scales = [jnp.exp2(p[1] - top) for p in parts]
    total = functools.reduce(jnp.add, scales)
    out = functools.reduce(jnp.add, [p[0] * (s / total) for p, s in zip(parts, scales)])
    return out, top + jnp.log2(total)


def masked(part, flag):
    return part[0], jnp.where(flag != 0, part[1], NEG)


def merge_kernel(part_flags, n_after, heads, flags, *refs):
    refs = refs[n_after:]
    n = len(part_flags)
    out, token = refs[n:]
    pass_flags(flags, token)
    for head in range(heads):
        write_part(
            out, head, *merge_parts([masked(read_part(refs[i], head), flags[f]) for i, f in enumerate(part_flags)])
        )


def merge(name, flags, own, h0, parts, part_flags, nh, step, flops, after):
    smem = pl.BlockSpec(memory_space=pltpu.SMEM)
    block = pl.BlockSpec((step * BLOCK, TILE), lambda h: (h, 0))
    res = pl.pallas_call(
        functools.partial(merge_kernel, part_flags, len(after), step),
        grid=(nh // step,),
        in_specs=[smem] + [pl.BlockSpec(memory_space=pl.ANY)] * len(after)
        + [pl.BlockSpec((step * BLOCK, TILE), lambda h: (h + h0 // step, 0))]
        + [block] * len(parts),
        out_specs=[block, smem],
        out_shape=[
            jax.ShapeDtypeStruct((nh * BLOCK, TILE), BF),
            jax.ShapeDtypeStruct(flags.shape, flags.dtype),
        ],
        compiler_params=pltpu.CompilerParams(vmem_limit_bytes=VMEM),
        cost_estimate=pl.CostEstimate(flops=flops, bytes_accessed=1000, transcendentals=0),
        name=name,
    )(flags, *after, own, *parts)
    return res[1], res[0]


def side_kernel(heads, flags, q_ref, kv_ref, lo_ref, hi_ref, out_ref, token):
    pass_flags(flags, token)

    def get(head, _):
        at = lanes(head)
        keys = jnp.concatenate([kv_ref[t, 0, :, at] for t in range(TT)], axis=0)
        values = jnp.concatenate([kv_ref[t, 1, :, at].T for t in range(TT)], axis=1)
        return q_ref[:, at], keys, values

    def finish(head, _, out, log):
        parts = [masked((out, log), flags[3])]
        parts += [masked(read_part(r, head), flags[f]) for r, f in ((lo_ref, 4), (hi_ref, 5))]
        write_part(out_ref, head, *merge_parts(parts))

    attend_all(heads, 1, get, finish)


def side_and_merge(flags, q, kv, parts, h0, nh, step, flops):
    smem = pl.BlockSpec(memory_space=pltpu.SMEM)
    block = pl.BlockSpec((step * BLOCK, TILE), lambda h: (h, 0))
    base = h0 // step
    res = pl.pallas_call(
        functools.partial(side_kernel, step),
        grid=(nh // step,),
        in_specs=[
            smem,
            pl.BlockSpec((TILE, step * HD), lambda h: (0, h + base)),
            pl.BlockSpec((TT, 2, TILE, step * HD), lambda h: (0, 0, 0, h + base)),
            block,
            block,
        ],
        out_specs=[block, smem],
        out_shape=[
            jax.ShapeDtypeStruct((nh * BLOCK, TILE), BF),
            jax.ShapeDtypeStruct(flags.shape, flags.dtype),
        ],
        compiler_params=pltpu.CompilerParams(vmem_limit_bytes=VMEM),
        cost_estimate=pl.CostEstimate(flops=flops, bytes_accessed=1000, transcendentals=0),
        name="side",
    )(flags, q, kv, *parts)
    return res[1], res[0]


def far_kernel(width, h0, nh, heads, flags, offsets, q_ref, tiles, *refs):
    out_ref, token, buffer, sems = refs[-4:]
    step = pl.program_id(0)
    pass_flags(flags, token)

    def copy(i):
        owner = lax.rem(flags[6] + 1 + offsets[h0 * FAR + i], width)
        cols = pl.ds(pl.multiple_of(h0 * HD + i // FAR * HD, HD), HD)
        return pltpu.make_async_copy(tiles.at[owner, :, :, cols], buffer.at[i], sems.at[i])

    @pl.when(step == 0)
    def _():
        @pl.loop(0, nh * FAR)
        def _(i):
            copy(i).start()

    for i in range(heads * FAR):
        copy(step * (heads * FAR) + i).wait()

    def get(head, _):
        first = (step * heads + head) * FAR
        keys = jnp.concatenate([buffer[first + f, 0] for f in range(FAR)], axis=0)
        values = jnp.concatenate([buffer[first + f, 1].T for f in range(FAR)], axis=1)
        return q_ref[:, lanes(head)], keys, values

    attend_all(heads, 1, get, lambda head, _, out, log: write_part(out_ref, head, out, log))


def far(flags, offsets, q, tiles, h0, nh, step, flops, after):
    smem = pl.BlockSpec(memory_space=pltpu.SMEM)
    res = pl.pallas_call(
        functools.partial(far_kernel, tiles.shape[0], h0, nh, step),
        grid=(nh // step,),
        in_specs=[
            smem, smem, pl.BlockSpec((TILE, step * HD), lambda h: (0, h + h0 // step))
        ] + [pl.BlockSpec(memory_space=pl.ANY)] * (1 + len(after)),
        out_specs=[pl.BlockSpec((step * BLOCK, TILE), lambda h: (h, 0)), smem],
        out_shape=[
            jax.ShapeDtypeStruct((nh * BLOCK, TILE), F32),
            jax.ShapeDtypeStruct(flags.shape, flags.dtype),
        ],
        scratch_shapes=[
            pltpu.VMEM((nh * FAR, 2, TILE, HD), BF),
            pltpu.SemaphoreType.DMA((nh * FAR,)),
        ],
        compiler_params=pltpu.CompilerParams(vmem_limit_bytes=VMEM),
        cost_estimate=pl.CostEstimate(flops=flops, bytes_accessed=1000, transcendentals=0),
        name="far",
    )(flags, offsets, q, tiles, *after)
    return res[1], res[0]


def final_kernel(part_flags, heads, flags, *refs):
    n = len(part_flags)
    arrays, out_ref, token = refs[:n], refs[-2], refs[-1]
    pass_flags(flags, token)
    for head in range(heads):
        parts = [masked(read_part(a, head), flags[f]) for a, f in zip(arrays, part_flags)]
        out_ref[:, lanes(head)] = merge_parts(parts)[0].T.astype(out_ref.dtype)


def final(flags, parts, h0, nh, step, out, flops):
    smem = pl.BlockSpec(memory_space=pltpu.SMEM)
    specs = [
        pl.BlockSpec((step * BLOCK, TILE), functools.partial(lambda h, d: (h + d, 0), d=(h0 - base) // step))
        for _, base, _ in parts
    ]
    before = [] if out is None else [out]
    return pl.pallas_call(
        functools.partial(final_kernel, [f for f, _, _ in parts], step),
        grid=(nh // step,),
        in_specs=[smem] + specs + [pl.BlockSpec(memory_space=pl.ANY)] * len(before),
        out_specs=[pl.BlockSpec((TILE, step * HD), lambda h: (0, h + h0 // step)), smem],
        out_shape=[
            jax.ShapeDtypeStruct((TILE, HEADS * HD), BF),
            jax.ShapeDtypeStruct(flags.shape, flags.dtype),
        ],
        input_output_aliases={} if out is None else {1 + len(parts): 0},
        compiler_params=pltpu.CompilerParams(vmem_limit_bytes=VMEM),
        cost_estimate=pl.CostEstimate(flops=flops, bytes_accessed=1000, transcendentals=0),
        name="final",
    )(flags, *[a for _, _, a in parts], *before)


def on_device(queries, keys_values, far_offsets):
    width, height = lax.axis_size("wa"), lax.axis_size("ha")
    col, row = lax.axis_index("wa"), lax.axis_index("ha")
    up = [(i, i + 1) for i in range(height - 1)]
    down = [(j, i) for i, j in up]
    mate = [(i, i ^ 1) for i in range(width)]
    across = [(i, i + 1) for i in range(1, width - 1, 2)]
    across = across + [(j, i) for i, j in across]

    q = queries.reshape(TILE, HEADS * HD)
    kv = keys_values.reshape(TT, 2, TILE, HEADS * HD)

    lo, hi = row > 0, row < height - 1
    side = (col > 0) & (col < width - 1)
    flags = jnp.stack(
        [jnp.int32(1)] + [f.astype(jnp.int32) for f in (lo, hi, side, side & lo, side & hi)] + [col, row]
    )

    kv_mate = lax.ppermute(kv, "wa", mate)
    q_side = lax.ppermute(q, "wa", across)
    q_lo = lax.ppermute(q, "ha", up)
    q_hi = lax.ppermute(q, "ha", down)
    middle = kv[1]

    flags, (own,) = window("own", flags, [q], [kv, kv_mate], [(0, (0, 1))], 0, HEADS, [F32], 1, 3, after=[middle])
    tiles = lax.all_gather(middle, "wa")
    q_side, flags = lax.optimization_barrier((q_side, flags))
    qs_lo = lax.ppermute(q_side, "ha", up)
    qs_hi = lax.ppermute(q_side, "ha", down)

    def side_rows(flags, g, flops):
        flags, (s_lo, s_hi) = window(
            "side_rows", flags, [qs_lo, qs_hi], [kv], [(0, (0,)), (1, (0,))], *GROUPS[g], [BF, BF], 2, 2, flops
        )
        return flags, [lax.ppermute(s_hi, "ha", up), lax.ppermute(s_lo, "ha", down)]

    flags, (o_lo, o_hi) = window(
        "rows", flags, [q_lo, q_hi], [kv, kv_mate], [(0, (0, 1)), (1, (0, 1))], 0, HEADS, [BF, BF], 2, 2, 10**13
    )
    flags, (s_own,) = window("side_own", flags, [q_side], [kv], [(0, (0,))], *GROUPS[0], [F32], 1, 3)
    flags, first = side_rows(flags, 0, 1000)
    flags, second = side_rows(flags, 1, 1000)
    o_lo, o_hi, flags = lax.optimization_barrier((o_lo, o_hi, flags))
    from_lo = lax.ppermute(o_hi, "ha", up)
    from_hi = lax.ppermute(o_lo, "ha", down)
    flags, first = merge("side_merge", flags, s_own, 0, first, [3, 4, 5], GROUPS[0][1], 6, 1000, [])
    first = lax.ppermute(first, "wa", across)
    flags, second = side_and_merge(flags, q_side, kv, second, *GROUPS[1], 3, 8 * 10**9)
    second = lax.ppermute(second, "wa", across)
    offsets = far_offsets.reshape(-1)
    flags, far_first = far(flags, offsets, q, tiles, *GROUPS[0], 3, 1000, [])
    flags, far_second = far(flags, offsets, q, tiles, *GROUPS[1], 3, 1000, [])
    out = None
    for (low, count), side_merged, far_part, flops in zip(
        GROUPS, (first, second), (far_first, far_second), (30 * 10**9, 1000)
    ):
        out, flags = final(
            flags,
            [(0, 0, own), (0, low, far_part), (1, 0, from_lo), (2, 0, from_hi), (3, low, side_merged)],
            low, count, 3, out, flops,
        )
    return out.reshape(queries.shape)


def solution(mesh):
    placed = (
        P("ha", "wa", None, None),
        P("ha", "wa", None, None, None, None),
        P("wa", "ha", None, None),
    )
    return jax.shard_map(
        on_device, mesh=mesh, in_specs=placed, out_specs=P("ha", "wa", None, None), check_vma=False
    )
```

```python
import functools

import jax
import jax.numpy as jnp
from jax import lax
from jax.experimental import pallas as pl
from jax.experimental.pallas import tpu as pltpu
from jax.sharding import PartitionSpec as P

HEADS = 12
HD = 128
TILE = 384
TT = 3
FAR = 2
NEG = -1e30
SCALE2 = 1.4426950408889634 / HD**0.5
VMEM = 127 * 2**19
GROUPS = ((0, 6), (6, 6))
BF, F32 = jnp.bfloat16, jnp.float32
LOG_ROWS = 16
BLOCK = HD + LOG_ROWS


SAMPLE = 128
LIMIT = 2.0**100


def attend(q, keys, values, peak):
    s = lax.dot_general(keys, q, (((1,), (1,)), ((), ())), preferred_element_type=F32)
    if peak is None:
        peak = jnp.max(s, axis=0, keepdims=True)
    weights = jnp.exp2((s - peak) * SCALE2)
    total = jnp.sum(weights, axis=0, keepdims=True)
    summed = jnp.dot(values, weights.astype(BF), preferred_element_type=F32)
    return summed, total, peak


def attend_all(heads, groups, get, finish):
    worst = None
    for head in range(heads):
        for group in range(groups):
            q, keys, values = get(head, group)
            some = lax.dot_general(
                keys[:SAMPLE], q, (((1,), (1,)), ((), ())), preferred_element_type=F32
            )
            peak = jnp.max(some, axis=0, keepdims=True)
            summed, total, _ = attend(q, keys, values, peak)
            finish(head, group, summed / total, peak * SCALE2 + jnp.log2(total))
            worst = total if worst is None else jnp.maximum(worst, total)

    @pl.when(jnp.logical_not(jnp.max(worst) < LIMIT))
    def _():
        @pl.loop(0, heads)
        def _(head):
            for group in range(groups):
                summed, total, peak = attend(*get(head, group), None)
                finish(head, group, summed / total, peak * SCALE2 + jnp.log2(total))


def rows_of(head, start, size):
    low = head * BLOCK + start
    return pl.ds(low if isinstance(head, int) else pl.multiple_of(low, 16), size)


def write_part(ref, head, out, log):
    first = log.astype(BF).astype(F32)
    second = (log - first).astype(BF).astype(F32)
    row = lax.broadcasted_iota(jnp.int32, (LOG_ROWS, log.shape[1]), 0)
    third = jnp.where(row == 2, log - first - second, 0.0)
    terms = jnp.where(row == 0, first, jnp.where(row == 1, second, third))
    ref[rows_of(head, 0, HD), :] = out.astype(ref.dtype)
    ref[rows_of(head, HD, LOG_ROWS), :] = terms.astype(ref.dtype)


def read_part(ref, head):
    log = jnp.sum(ref[rows_of(head, HD, LOG_ROWS), :].astype(F32), axis=0, keepdims=True)
    return ref[rows_of(head, 0, HD), :].astype(F32), log


def lanes(i):
    return pl.ds(i * HD if isinstance(i, int) else pl.multiple_of(i * HD, HD), HD)


def pass_flags(flags, token):
    for i in range(8):
        token[i] = flags[i]


def window_kernel(jobs, n_q, n_kv, n_after, join, heads, flags, *refs):
    refs = refs[n_after:]
    q_refs = refs[:n_q]
    kv_refs = refs[n_q : n_q + n_kv]
    outs = refs[n_q + n_kv : n_q + n_kv + len(jobs)]
    pass_flags(flags, refs[n_q + n_kv + len(jobs)])
    groups = [list(range(i, min(i + join, len(jobs)))) for i in range(0, len(jobs), join)]

    def get(head, group):
        at = lanes(head)
        kvs = [kv_refs[i] for i in jobs[groups[group][0]][1]]
        q = jnp.concatenate([q_refs[jobs[j][0]][:, at] for j in groups[group]], axis=0)
        keys = jnp.concatenate([kv[t, 0, :, at] for kv in kvs for t in range(TT)], axis=0)
        values = jnp.concatenate([kv[t, 1, :, at].T for kv in kvs for t in range(TT)], axis=1)
        return q, keys, values

    def finish(head, group, out, log):
        for k, j in enumerate(groups[group]):
            cut = slice(k * TILE, (k + 1) * TILE)
            write_part(outs[j], head, out[:, cut], log[:, cut])

    attend_all(heads, len(groups), get, finish)


def window(name, flags, qs, kvs, jobs, h0, nh, out_types, join, step, flops=1000, after=()):
    smem = pl.BlockSpec(memory_space=pltpu.SMEM)
    base = h0 // step
    specs = [smem] + [pl.BlockSpec(memory_space=pl.ANY) for _ in after]
    specs += [pl.BlockSpec((TILE, step * HD), lambda h: (0, h + base)) for _ in qs]
    specs += [pl.BlockSpec((TT, 2, TILE, step * HD), lambda h: (0, 0, 0, h + base)) for _ in kvs]
    res = pl.pallas_call(
        functools.partial(window_kernel, jobs, len(qs), len(kvs), len(after), join, step),
        grid=(nh // step,),
        in_specs=specs,
        out_specs=[pl.BlockSpec((step * BLOCK, TILE), lambda h: (h, 0)) for _ in jobs] + [smem],
        out_shape=[jax.ShapeDtypeStruct((nh * BLOCK, TILE), t) for t in out_types]
        + [jax.ShapeDtypeStruct(flags.shape, flags.dtype)],
        compiler_params=pltpu.CompilerParams(vmem_limit_bytes=VMEM),
        cost_estimate=pl.CostEstimate(flops=flops, bytes_accessed=1000, transcendentals=0),
        name=name,
    )(flags, *after, *qs, *kvs)
    return res[-1], res[:-1]


def merge_parts(parts):
    top = functools.reduce(jnp.maximum, [p[1] for p in parts])
    scales = [jnp.exp2(p[1] - top) for p in parts]
    total = functools.reduce(jnp.add, scales)
    out = functools.reduce(jnp.add, [p[0] * (s / total) for p, s in zip(parts, scales)])
    return out, top + jnp.log2(total)


def masked(part, flag):
    return part[0], jnp.where(flag != 0, part[1], NEG)


def side_kernel(heads, flags, q_ref, kv_ref, lo_ref, hi_ref, out_ref, token):
    pass_flags(flags, token)

    def get(head, _):
        at = lanes(head)
        keys = jnp.concatenate([kv_ref[t, 0, :, at] for t in range(TT)], axis=0)
        values = jnp.concatenate([kv_ref[t, 1, :, at].T for t in range(TT)], axis=1)
        return q_ref[:, at], keys, values

    def finish(head, _, out, log):
        parts = [masked((out, log), flags[3])]
        parts += [masked(read_part(r, head), flags[f]) for r, f in ((lo_ref, 4), (hi_ref, 5))]
        write_part(out_ref, head, *merge_parts(parts))

    attend_all(heads, 1, get, finish)


def side_and_merge(flags, q, kv, parts, h0, nh, step, flops):
    smem = pl.BlockSpec(memory_space=pltpu.SMEM)
    block = pl.BlockSpec((step * BLOCK, TILE), lambda h: (h, 0))
    base = h0 // step
    res = pl.pallas_call(
        functools.partial(side_kernel, step),
        grid=(nh // step,),
        in_specs=[
            smem,
            pl.BlockSpec((TILE, step * HD), lambda h: (0, h + base)),
            pl.BlockSpec((TT, 2, TILE, step * HD), lambda h: (0, 0, 0, h + base)),
            block,
            block,
        ],
        out_specs=[block, smem],
        out_shape=[
            jax.ShapeDtypeStruct((nh * BLOCK, TILE), BF),
            jax.ShapeDtypeStruct(flags.shape, flags.dtype),
        ],
        compiler_params=pltpu.CompilerParams(vmem_limit_bytes=VMEM),
        cost_estimate=pl.CostEstimate(flops=flops, bytes_accessed=1000, transcendentals=0),
        name="side",
    )(flags, q, kv, *parts)
    return res[1], res[0]


def far_kernel(width, h0, nh, heads, flags, offsets, q_ref, tiles, *refs):
    out_ref, token, buffer, sems = refs[-4:]
    step = pl.program_id(0)
    pass_flags(flags, token)

    def copy(i):
        owner = lax.rem(flags[6] + 1 + offsets[h0 * FAR + i], width)
        cols = pl.ds(pl.multiple_of(h0 * HD + i // FAR * HD, HD), HD)
        return pltpu.make_async_copy(tiles.at[owner, :, :, cols], buffer.at[i], sems.at[i])

    @pl.when(step == 0)
    def _():
        @pl.loop(0, nh * FAR)
        def _(i):
            copy(i).start()

    for i in range(heads * FAR):
        copy(step * (heads * FAR) + i).wait()

    def get(head, _):
        first = (step * heads + head) * FAR
        keys = jnp.concatenate([buffer[first + f, 0] for f in range(FAR)], axis=0)
        values = jnp.concatenate([buffer[first + f, 1].T for f in range(FAR)], axis=1)
        return q_ref[:, lanes(head)], keys, values

    attend_all(heads, 1, get, lambda head, _, out, log: write_part(out_ref, head, out, log))


def far(flags, offsets, q, tiles, h0, nh, step, flops, after):
    smem = pl.BlockSpec(memory_space=pltpu.SMEM)
    res = pl.pallas_call(
        functools.partial(far_kernel, tiles.shape[0], h0, nh, step),
        grid=(nh // step,),
        in_specs=[
            smem, smem, pl.BlockSpec((TILE, step * HD), lambda h: (0, h + h0 // step))
        ] + [pl.BlockSpec(memory_space=pl.ANY)] * (1 + len(after)),
        out_specs=[pl.BlockSpec((step * BLOCK, TILE), lambda h: (h, 0)), smem],
        out_shape=[
            jax.ShapeDtypeStruct((nh * BLOCK, TILE), F32),
            jax.ShapeDtypeStruct(flags.shape, flags.dtype),
        ],
        scratch_shapes=[
            pltpu.VMEM((nh * FAR, 2, TILE, HD), BF),
            pltpu.SemaphoreType.DMA((nh * FAR,)),
        ],
        compiler_params=pltpu.CompilerParams(vmem_limit_bytes=VMEM),
        cost_estimate=pl.CostEstimate(flops=flops, bytes_accessed=1000, transcendentals=0),
        name="far",
    )(flags, offsets, q, tiles, *after)
    return res[1], res[0]


def final_kernel(part_flags, heads, flags, *refs):
    n = len(part_flags)
    arrays, out_ref, token = refs[:n], refs[-2], refs[-1]
    pass_flags(flags, token)
    for head in range(heads):
        parts = [masked(read_part(a, head), flags[f]) for a, f in zip(arrays, part_flags)]
        out_ref[:, lanes(head)] = merge_parts(parts)[0].T.astype(out_ref.dtype)


def final(flags, parts, h0, nh, step, out, flops):
    smem = pl.BlockSpec(memory_space=pltpu.SMEM)
    specs = [
        pl.BlockSpec((step * BLOCK, TILE), functools.partial(lambda h, d: (h + d, 0), d=(h0 - base) // step))
        for _, base, _ in parts
    ]
    before = [] if out is None else [out]
    return pl.pallas_call(
        functools.partial(final_kernel, [f for f, _, _ in parts], step),
        grid=(nh // step,),
        in_specs=[smem] + specs + [pl.BlockSpec(memory_space=pl.ANY)] * len(before),
        out_specs=[pl.BlockSpec((TILE, step * HD), lambda h: (0, h + h0 // step)), smem],
        out_shape=[
            jax.ShapeDtypeStruct((TILE, HEADS * HD), BF),
            jax.ShapeDtypeStruct(flags.shape, flags.dtype),
        ],
        input_output_aliases={} if out is None else {1 + len(parts): 0},
        compiler_params=pltpu.CompilerParams(vmem_limit_bytes=VMEM),
        cost_estimate=pl.CostEstimate(flops=flops, bytes_accessed=1000, transcendentals=0),
        name="final",
    )(flags, *[a for _, _, a in parts], *before)


def on_device(queries, keys_values, far_offsets):
    width, height = lax.axis_size("wa"), lax.axis_size("ha")
    col, row = lax.axis_index("wa"), lax.axis_index("ha")
    up = [(i, i + 1) for i in range(height - 1)]
    down = [(j, i) for i, j in up]
    mate = [(i, i ^ 1) for i in range(width)]
    across = [(i, i + 1) for i in range(1, width - 1, 2)]
    across = across + [(j, i) for i, j in across]

    q = queries.reshape(TILE, HEADS * HD)
    kv = keys_values.reshape(TT, 2, TILE, HEADS * HD)

    lo, hi = row > 0, row < height - 1
    side = (col > 0) & (col < width - 1)
    flags = jnp.stack(
        [jnp.int32(1)] + [f.astype(jnp.int32) for f in (lo, hi, side, side & lo, side & hi)] + [col, row]
    )

    kv_mate = lax.ppermute(kv, "wa", mate)
    q_side = lax.ppermute(q, "wa", across)
    q_lo = lax.ppermute(q, "ha", up)
    q_hi = lax.ppermute(q, "ha", down)
    middle = kv[1]

    flags, (own,) = window("own", flags, [q], [kv, kv_mate], [(0, (0, 1))], 0, HEADS, [F32], 1, 3, after=[middle])
    tiles = lax.all_gather(middle, "wa")
    q_side, flags = lax.optimization_barrier((q_side, flags))
    qs_lo = lax.ppermute(q_side, "ha", up)
    qs_hi = lax.ppermute(q_side, "ha", down)

    def side_rows(flags, g, flops):
        flags, (s_lo, s_hi) = window(
            "side_rows", flags, [qs_lo, qs_hi], [kv], [(0, (0,)), (1, (0,))], *GROUPS[g], [BF, BF], 2, 2, flops
        )
        return flags, [lax.ppermute(s_hi, "ha", up), lax.ppermute(s_lo, "ha", down)]

    flags, (o_lo, o_hi) = window(
        "rows", flags, [q_lo, q_hi], [kv, kv_mate], [(0, (0, 1)), (1, (0, 1))], 0, HEADS, [BF, BF], 2, 2, 10**13
    )
    flags, first = side_rows(flags, 0, 1000)
    flags, second = side_rows(flags, 1, 1000)
    o_lo, o_hi, flags = lax.optimization_barrier((o_lo, o_hi, flags))
    from_lo = lax.ppermute(o_hi, "ha", up)
    from_hi = lax.ppermute(o_lo, "ha", down)
    flags, first = side_and_merge(flags, q_side, kv, first, *GROUPS[0], 3, 1000)
    first = lax.ppermute(first, "wa", across)
    flags, second = side_and_merge(flags, q_side, kv, second, *GROUPS[1], 3, 8 * 10**9)
    second = lax.ppermute(second, "wa", across)
    offsets = far_offsets.reshape(-1)
    flags, far_part = far(flags, offsets, q, tiles, 0, HEADS, 3, 1000, [])
    out = None
    for (low, count), side_merged, flops in zip(GROUPS, (first, second), (30 * 10**9, 1000)):
        out, flags = final(
            flags,
            [(0, 0, own), (0, 0, far_part), (1, 0, from_lo), (2, 0, from_hi), (3, low, side_merged)],
            low, count, 3, out, flops,
        )
    return out.reshape(queries.shape)


def solution(mesh):
    placed = (
        P("ha", "wa", None, None),
        P("ha", "wa", None, None, None, None),
        P("wa", "ha", None, None),
    )
    return jax.shard_map(
        on_device, mesh=mesh, in_specs=placed, out_specs=P("ha", "wa", None, None), check_vma=False
    )
```

```python
import functools

import jax
import jax.numpy as jnp
from jax import lax
from jax.experimental import pallas as pl
from jax.experimental.pallas import tpu as pltpu
from jax.sharding import PartitionSpec as P

HEADS = 12
HD = 128
TILE = 384
TT = 3
FAR = 2
NEG = -1e30
SCALE2 = 1.4426950408889634 / HD**0.5
VMEM = 127 * 2**19
GROUPS = ((0, 6), (6, 6))
BF, F32 = jnp.bfloat16, jnp.float32
LOG_ROWS = 16
BLOCK = HD + LOG_ROWS


SAMPLE = 128
LIMIT = 2.0**100


def attend(q, keys, values, peak):
    s = lax.dot_general(keys, q, (((1,), (1,)), ((), ())), preferred_element_type=F32)
    if peak is None:
        peak = jnp.max(s, axis=0, keepdims=True)
    weights = jnp.exp2((s - peak) * SCALE2)
    total = jnp.sum(weights, axis=0, keepdims=True)
    summed = jnp.dot(values, weights.astype(BF), preferred_element_type=F32)
    return summed, total, peak


def attend_all(heads, groups, get, finish):
    worst = None
    for head in range(heads):
        for group in range(groups):
            q, keys, values = get(head, group)
            some = lax.dot_general(
                keys[:SAMPLE], q, (((1,), (1,)), ((), ())), preferred_element_type=F32
            )
            peak = jnp.max(some, axis=0, keepdims=True)
            summed, total, _ = attend(q, keys, values, peak)
            finish(head, group, summed / total, peak * SCALE2 + jnp.log2(total))
            worst = total if worst is None else jnp.maximum(worst, total)

    @pl.when(jnp.logical_not(jnp.max(worst) < LIMIT))
    def _():
        @pl.loop(0, heads)
        def _(head):
            for group in range(groups):
                summed, total, peak = attend(*get(head, group), None)
                finish(head, group, summed / total, peak * SCALE2 + jnp.log2(total))


def rows_of(head, start, size):
    low = head * BLOCK + start
    return pl.ds(low if isinstance(head, int) else pl.multiple_of(low, 16), size)


def write_part(ref, head, out, log):
    first = log.astype(BF).astype(F32)
    second = (log - first).astype(BF).astype(F32)
    row = lax.broadcasted_iota(jnp.int32, (LOG_ROWS, log.shape[1]), 0)
    third = jnp.where(row == 2, log - first - second, 0.0)
    terms = jnp.where(row == 0, first, jnp.where(row == 1, second, third))
    ref[rows_of(head, 0, HD), :] = out.astype(ref.dtype)
    ref[rows_of(head, HD, LOG_ROWS), :] = terms.astype(ref.dtype)


def read_part(ref, head):
    log = jnp.sum(ref[rows_of(head, HD, LOG_ROWS), :].astype(F32), axis=0, keepdims=True)
    return ref[rows_of(head, 0, HD), :].astype(F32), log


def lanes(i):
    return pl.ds(i * HD if isinstance(i, int) else pl.multiple_of(i * HD, HD), HD)


def pass_flags(flags, token):
    for i in range(8):
        token[i] = flags[i]


def window_kernel(jobs, n_q, n_kv, n_after, join, heads, flags, *refs):
    refs = refs[n_after:]
    q_refs = refs[:n_q]
    kv_refs = refs[n_q : n_q + n_kv]
    outs = refs[n_q + n_kv : n_q + n_kv + len(jobs)]
    pass_flags(flags, refs[n_q + n_kv + len(jobs)])
    groups = [list(range(i, min(i + join, len(jobs)))) for i in range(0, len(jobs), join)]

    def get(head, group):
        at = lanes(head)
        kvs = [kv_refs[i] for i in jobs[groups[group][0]][1]]
        q = jnp.concatenate([q_refs[jobs[j][0]][:, at] for j in groups[group]], axis=0)
        keys = jnp.concatenate([kv[t, 0, :, at] for kv in kvs for t in range(TT)], axis=0)
        values = jnp.concatenate([kv[t, 1, :, at].T for kv in kvs for t in range(TT)], axis=1)
        return q, keys, values

    def finish(head, group, out, log):
        for k, j in enumerate(groups[group]):
            cut = slice(k * TILE, (k + 1) * TILE)
            write_part(outs[j], head, out[:, cut], log[:, cut])

    attend_all(heads, len(groups), get, finish)


def window(name, flags, qs, kvs, jobs, h0, nh, out_types, join, step, flops=1000, after=()):
    smem = pl.BlockSpec(memory_space=pltpu.SMEM)
    base = h0 // step
    specs = [smem] + [pl.BlockSpec(memory_space=pl.ANY) for _ in after]
    specs += [pl.BlockSpec((TILE, step * HD), lambda h: (0, h + base)) for _ in qs]
    specs += [pl.BlockSpec((TT, 2, TILE, step * HD), lambda h: (0, 0, 0, h + base)) for _ in kvs]
    res = pl.pallas_call(
        functools.partial(window_kernel, jobs, len(qs), len(kvs), len(after), join, step),
        grid=(nh // step,),
        in_specs=specs,
        out_specs=[pl.BlockSpec((step * BLOCK, TILE), lambda h: (h, 0)) for _ in jobs] + [smem],
        out_shape=[jax.ShapeDtypeStruct((nh * BLOCK, TILE), t) for t in out_types]
        + [jax.ShapeDtypeStruct(flags.shape, flags.dtype)],
        compiler_params=pltpu.CompilerParams(vmem_limit_bytes=VMEM),
        cost_estimate=pl.CostEstimate(flops=flops, bytes_accessed=1000, transcendentals=0),
        name=name,
    )(flags, *after, *qs, *kvs)
    return res[-1], res[:-1]


def merge_parts(parts):
    top = functools.reduce(jnp.maximum, [p[1] for p in parts])
    scales = [jnp.exp2(p[1] - top) for p in parts]
    total = functools.reduce(jnp.add, scales)
    out = functools.reduce(jnp.add, [p[0] * (s / total) for p, s in zip(parts, scales)])
    return out, top + jnp.log2(total)


def masked(part, flag):
    return part[0], jnp.where(flag != 0, part[1], NEG)


def side_kernel(heads, flags, q_ref, kv_ref, lo_ref, hi_ref, out_ref, token):
    pass_flags(flags, token)

    def get(head, _):
        at = lanes(head)
        keys = jnp.concatenate([kv_ref[t, 0, :, at] for t in range(TT)], axis=0)
        values = jnp.concatenate([kv_ref[t, 1, :, at].T for t in range(TT)], axis=1)
        return q_ref[:, at], keys, values

    def finish(head, _, out, log):
        parts = [masked((out, log), flags[3])]
        parts += [masked(read_part(r, head), flags[f]) for r, f in ((lo_ref, 4), (hi_ref, 5))]
        write_part(out_ref, head, *merge_parts(parts))

    attend_all(heads, 1, get, finish)


def side_and_merge(flags, q, kv, parts, h0, nh, step, flops):
    smem = pl.BlockSpec(memory_space=pltpu.SMEM)
    block = pl.BlockSpec((step * BLOCK, TILE), lambda h: (h, 0))
    base = h0 // step
    res = pl.pallas_call(
        functools.partial(side_kernel, step),
        grid=(nh // step,),
        in_specs=[
            smem,
            pl.BlockSpec((TILE, step * HD), lambda h: (0, h + base)),
            pl.BlockSpec((TT, 2, TILE, step * HD), lambda h: (0, 0, 0, h + base)),
            block,
            block,
        ],
        out_specs=[block, smem],
        out_shape=[
            jax.ShapeDtypeStruct((nh * BLOCK, TILE), BF),
            jax.ShapeDtypeStruct(flags.shape, flags.dtype),
        ],
        compiler_params=pltpu.CompilerParams(vmem_limit_bytes=VMEM),
        cost_estimate=pl.CostEstimate(flops=flops, bytes_accessed=1000, transcendentals=0),
        name="side",
    )(flags, q, kv, *parts)
    return res[1], res[0]


def far_kernel(width, h0, nh, heads, flags, offsets, q_ref, tiles, *refs):
    out_ref, token, buffer, sems = refs[-4:]
    step = pl.program_id(0)
    pass_flags(flags, token)

    def copy(i):
        owner = lax.rem(flags[6] + 1 + offsets[h0 * FAR + i], width)
        cols = pl.ds(pl.multiple_of(h0 * HD + i // FAR * HD, HD), HD)
        return pltpu.make_async_copy(tiles.at[owner, :, :, cols], buffer.at[i], sems.at[i])

    @pl.when(step == 0)
    def _():
        @pl.loop(0, nh * FAR)
        def _(i):
            copy(i).start()

    for i in range(heads * FAR):
        copy(step * (heads * FAR) + i).wait()

    def get(head, _):
        first = (step * heads + head) * FAR
        keys = jnp.concatenate([buffer[first + f, 0] for f in range(FAR)], axis=0)
        values = jnp.concatenate([buffer[first + f, 1].T for f in range(FAR)], axis=1)
        return q_ref[:, lanes(head)], keys, values

    attend_all(heads, 1, get, lambda head, _, out, log: write_part(out_ref, head, out, log))


def far(flags, offsets, q, tiles, h0, nh, step, flops, after):
    smem = pl.BlockSpec(memory_space=pltpu.SMEM)
    res = pl.pallas_call(
        functools.partial(far_kernel, tiles.shape[0], h0, nh, step),
        grid=(nh // step,),
        in_specs=[
            smem, smem, pl.BlockSpec((TILE, step * HD), lambda h: (0, h + h0 // step))
        ] + [pl.BlockSpec(memory_space=pl.ANY)] * (1 + len(after)),
        out_specs=[pl.BlockSpec((step * BLOCK, TILE), lambda h: (h, 0)), smem],
        out_shape=[
            jax.ShapeDtypeStruct((nh * BLOCK, TILE), F32),
            jax.ShapeDtypeStruct(flags.shape, flags.dtype),
        ],
        scratch_shapes=[
            pltpu.VMEM((nh * FAR, 2, TILE, HD), BF),
            pltpu.SemaphoreType.DMA((nh * FAR,)),
        ],
        compiler_params=pltpu.CompilerParams(vmem_limit_bytes=VMEM),
        cost_estimate=pl.CostEstimate(flops=flops, bytes_accessed=1000, transcendentals=0),
        name="far",
    )(flags, offsets, q, tiles, *after)
    return res[1], res[0]


def final_kernel(part_flags, heads, flags, *refs):
    n = len(part_flags)
    arrays, out_ref, token = refs[:n], refs[-2], refs[-1]
    pass_flags(flags, token)
    for head in range(heads):
        parts = [masked(read_part(a, head), flags[f]) for a, f in zip(arrays, part_flags)]
        out_ref[:, lanes(head)] = merge_parts(parts)[0].T.astype(out_ref.dtype)


def final(flags, parts, h0, nh, step, out, flops):
    smem = pl.BlockSpec(memory_space=pltpu.SMEM)
    specs = [
        pl.BlockSpec((step * BLOCK, TILE), functools.partial(lambda h, d: (h + d, 0), d=(h0 - base) // step))
        for _, base, _ in parts
    ]
    before = [] if out is None else [out]
    return pl.pallas_call(
        functools.partial(final_kernel, [f for f, _, _ in parts], step),
        grid=(nh // step,),
        in_specs=[smem] + specs + [pl.BlockSpec(memory_space=pl.ANY)] * len(before),
        out_specs=[pl.BlockSpec((TILE, step * HD), lambda h: (0, h + h0 // step)), smem],
        out_shape=[
            jax.ShapeDtypeStruct((TILE, HEADS * HD), BF),
            jax.ShapeDtypeStruct(flags.shape, flags.dtype),
        ],
        input_output_aliases={} if out is None else {1 + len(parts): 0},
        compiler_params=pltpu.CompilerParams(vmem_limit_bytes=VMEM),
        cost_estimate=pl.CostEstimate(flops=flops, bytes_accessed=1000, transcendentals=0),
        name="final",
    )(flags, *[a for _, _, a in parts], *before)


def on_device(queries, keys_values, far_offsets):
    width, height = lax.axis_size("wa"), lax.axis_size("ha")
    col, row = lax.axis_index("wa"), lax.axis_index("ha")
    up = [(i, i + 1) for i in range(height - 1)]
    down = [(j, i) for i, j in up]
    mate = [(i, i ^ 1) for i in range(width)]
    across = [(i, i + 1) for i in range(1, width - 1, 2)]
    across = across + [(j, i) for i, j in across]

    q = queries.reshape(TILE, HEADS * HD)
    kv = keys_values.reshape(TT, 2, TILE, HEADS * HD)

    lo, hi = row > 0, row < height - 1
    side = (col > 0) & (col < width - 1)
    flags = jnp.stack(
        [jnp.int32(1)] + [f.astype(jnp.int32) for f in (lo, hi, side, side & lo, side & hi)] + [col, row]
    )

    kv_mate = lax.ppermute(kv, "wa", mate)
    q_side = lax.ppermute(q, "wa", across)
    q_lo = lax.ppermute(q, "ha", up)
    q_hi = lax.ppermute(q, "ha", down)
    middle = kv[1]
    offsets = far_offsets.reshape(-1)

    flags, (own,) = window("own", flags, [q], [kv, kv_mate], [(0, (0, 1))], 0, HEADS, [F32], 1, 3, after=[middle, offsets])
    tiles = lax.all_gather(middle, "wa")
    q_side, flags = lax.optimization_barrier((q_side, flags))
    qs_lo = lax.ppermute(q_side, "ha", up)
    qs_hi = lax.ppermute(q_side, "ha", down)

    def side_rows(flags, g, flops):
        flags, (s_lo, s_hi) = window(
            "side_rows", flags, [qs_lo, qs_hi], [kv], [(0, (0,)), (1, (0,))], *GROUPS[g], [BF, BF], 2, 2, flops
        )
        return flags, [lax.ppermute(s_hi, "ha", up), lax.ppermute(s_lo, "ha", down)]

    flags, (o_lo, o_hi) = window(
        "rows", flags, [q_lo, q_hi], [kv, kv_mate], [(0, (0, 1)), (1, (0, 1))], 0, HEADS, [BF, BF], 2, 2, 10**13
    )
    flags, first = side_rows(flags, 0, 1000)
    flags, second = side_rows(flags, 1, 1000)
    o_lo, o_hi, flags = lax.optimization_barrier((o_lo, o_hi, flags))
    from_lo = lax.ppermute(o_hi, "ha", up)
    from_hi = lax.ppermute(o_lo, "ha", down)
    flags, first = side_and_merge(flags, q_side, kv, first, *GROUPS[0], 3, 1000)
    first = lax.ppermute(first, "wa", across)
    flags, second = side_and_merge(flags, q_side, kv, second, *GROUPS[1], 3, 8 * 10**9)
    second = lax.ppermute(second, "wa", across)
    flags, far_part = far(flags, offsets, q, tiles, 0, HEADS, 3, 1000, [])
    out = None
    for (low, count), side_merged, flops in zip(GROUPS, (first, second), (30 * 10**9, 1000)):
        out, flags = final(
            flags,
            [(0, 0, own), (0, 0, far_part), (1, 0, from_lo), (2, 0, from_hi), (3, low, side_merged)],
            low, count, 3, out, flops,
        )
    return out.reshape(queries.shape)


def solution(mesh):
    placed = (
        P("ha", "wa", None, None),
        P("ha", "wa", None, None, None, None),
        P("wa", "ha", None, None),
    )
    return jax.shard_map(
        on_device, mesh=mesh, in_specs=placed, out_specs=P("ha", "wa", None, None), check_vma=False
    )
```
